32 devices in a mesh: grp: 2 (over y), shot: 4 (over z), sub: 4 (over x, core).
Axes of the slice: x: 2, y: 2, z: 4, core: 2. Of those that a mesh axis runs over, the one named last changes fastest.
Arguments:
- velocity: float32 [64, 64, 256], P(('grp', 'shot'), 'sub'), parts along dimension 0, may hold values from 1.5 to 4.5
- anchors: int32 [8], P(('grp', 'shot')), parts along dimension 0, may hold values from 0 to 3, as said below
- source_cells: int32 [8, 3], P(('grp', 'shot')), parts along dimension 0, may hold values from 0 to 255, as said below
- receiver_cells: int32 [8, 3, 256], P(('grp', 'shot')), parts along dimension 0, may hold values from 0 to 255, as said below
- wavelet: float32 [8, 2], P(('grp', 'shot')), parts along dimension 0, may hold values from -6 to 6
- residuals: float32 [8, 2, 256], P(('grp', 'shot')), parts along dimension 0, may hold values from -6 to 6
- forward_pair: float32 [8, 2, 32, 64, 256], P(('grp', 'shot'), None, None, 'sub'), parts along dimension 0, may hold values from -6 to 6
- adjoint_pair: float32 [8, 2, 32, 64, 256], P(('grp', 'shot'), None, None, 'sub'), parts along dimension 0, may hold values from -6 to 6
Outputs:
- gradient: float32 [64, 64, 256], P(('grp', 'shot'), 'sub'), parts along dimension 0
- forward_out: float32 [8, 2, 32, 64, 256], P(('grp', 'shot'), None, None, 'sub'), parts along dimension 0
- adjoint_out: float32 [8, 2, 32, 64, 256], P(('grp', 'shot'), None, None, 'sub'), parts along dimension 0
The draws below stay inside these ranges and needn't reach their ends.
There are 2 independent parts, one for each index of `grp`. The reference program is written for one: setup_inputs(seed, part) draws one part's arguments, and reference() takes and returns one part's arrays. A program takes and returns all parts, laid end to end along the dimension named above; each array names one. Nothing has to cross between parts.
Inputs may be any that keep to these rules, and one draw needn't show every extreme that they name: anchors[s] = (s - k) mod 4 for some k between 0 and 3. `source_cells`: entries are an aperture first index below 32, a depth below 64 and a y index below 256. `receiver_cells`: entries are an aperture first index below 32, a depth below 16 and a y index below 256; cells may repeat.
All inputs are finite; a program needn't handle non-finite values.
Results may differ from the reference program's by a relative error of at most 0.0003.
Values sent between devices are 32-bit elements; how exact they have to be, the bound alone decides.
No kernel may reach another device: no remote copies, remote signals or barrier semaphores. Data moves between devices by JAX's collectives and lax.ppermute only.
A program may use at most 64 MiB of HBM per device.

```python
import jax
import jax.numpy as jnp
from jax import lax

TX = 8
APT = 4
ZD = 16
MY = 256
NREC = 256
STEPS = 2
AX = 32
MX = 32
NZ = 64
N_SHOT = 4


def draw_anchors(key, part):
    key = jax.random.fold_in(key, 11)
    shots = jnp.arange(N_SHOT, dtype=jnp.int32)
    back = jax.random.randint(key, (N_SHOT,), 0, APT).astype(jnp.int32)
    back = jnp.where(shots < 2, 1, back).astype(jnp.int32)
    return ((shots - back + N_SHOT) % N_SHOT).astype(jnp.int32)


def draw_source_cells(key, part):
    key = jax.random.fold_in(key, 23)
    first_key, depth_key, side_key = jax.random.split(key, 3)
    first = jax.random.randint(first_key, (N_SHOT,), 0, AX)
    depth = jax.random.randint(depth_key, (N_SHOT,), 0, NZ)
    side = jax.random.randint(side_key, (N_SHOT,), 0, MY)
    return jnp.stack([first, depth, side], axis=1).astype(jnp.int32)


def draw_receiver_cells(key, part):
    key = jax.random.fold_in(key, 37)
    first_key, depth_key, side_key = jax.random.split(key, 3)
    first = jax.random.randint(first_key, (N_SHOT, NREC), 0, AX)
    depth = jax.random.randint(depth_key, (N_SHOT, NREC), 0, ZD)
    side = jax.random.randint(side_key, (N_SHOT, NREC), 0, MY)
    return jnp.stack([first, depth, side], axis=1).astype(jnp.int32)


def block_levels(rng, extent, cuts, least, largest):
    gain, own = 1.0, jax.random.fold_in(rng, 6)
    for position, parts in cuts:
        heights = jnp.exp(jax.random.uniform(jax.random.fold_in(own, position), (parts,), jnp.float32, least / len(cuts), largest / len(cuts)))
        gain = gain * jnp.repeat(heights, extent[position] // parts).reshape([-1 if axis == position else 1 for axis in range(len(extent))])
    return gain


def centred(key, extent, deviation, most, cuts=(), held_as=jnp.bfloat16):
    values = deviation * jax.random.normal(key, extent, jnp.float32)
    if cuts:
        values = values * block_levels(key, extent, cuts, -0.22, 0.18)
    return jnp.clip(values, -most, most).astype(held_as)


def setup_inputs(seed: int = 0, part: int = 0) -> dict:
    seeds = jax.random.split(jax.random.key(seed), 9)
    part_keys = jax.random.split(jax.random.fold_in(seeds[8], part), 9)
    velocity = jnp.clip(1.5 + 3.0 * jax.random.uniform(part_keys[0], (MX, NZ, MY), jnp.float32) ** block_levels(part_keys[0], (MX, NZ, MY), ((0, 4), (1, 4)), -0.2, 0.2), 1.5, 4.5)
    anchors = draw_anchors(jax.random.fold_in(jax.random.fold_in(seeds[8], part), 71), part)
    source_cells = draw_source_cells(jax.random.fold_in(jax.random.fold_in(seeds[8], part), 71), part)
    receiver_cells = draw_receiver_cells(jax.random.fold_in(jax.random.fold_in(seeds[8], part), 71), part)
    wavelet = centred(part_keys[4], (N_SHOT, STEPS), 1.0, 6.0, ((0, 4),), jnp.float32)
    residuals = centred(part_keys[5], (N_SHOT, STEPS, NREC), 1.0, 6.0, ((0, 4),), jnp.float32)
    forward_pair = centred(part_keys[6], (N_SHOT, 2, AX, NZ, MY), 1.0, 6.0, ((0, 4), (3, 4)), jnp.float32)
    adjoint_pair = centred(part_keys[7], (N_SHOT, 2, AX, NZ, MY), 1.0, 6.0, ((0, 4), (3, 4)), jnp.float32)
    return dict(velocity=velocity, anchors=anchors, source_cells=source_cells, receiver_cells=receiver_cells, wavelet=wavelet, residuals=residuals, forward_pair=forward_pair, adjoint_pair=adjoint_pair)


STENCIL_COEFS = (-205.0 / 72.0, 8.0 / 5.0, -1.0 / 5.0, 8.0 / 315.0, -1.0 / 560.0)
SPACING_RATIO = 0.1


def stencil(padded, field):
    rows_x, rows_z, rows_y = field.shape[-3:]
    total = 3.0 * STENCIL_COEFS[0] * field
    for offset in range(1, 5):
        along_x = padded[..., 4 + offset:4 + offset + rows_x, 4:4 + rows_z, 4:4 + rows_y] + padded[..., 4 - offset:4 - offset + rows_x, 4:4 + rows_z, 4:4 + rows_y]
        along_z = padded[..., 4:4 + rows_x, 4 + offset:4 + offset + rows_z, 4:4 + rows_y] + padded[..., 4:4 + rows_x, 4 - offset:4 - offset + rows_z, 4:4 + rows_y]
        along_y = padded[..., 4:4 + rows_x, 4:4 + rows_z, 4 + offset:4 + offset + rows_y] + padded[..., 4:4 + rows_x, 4:4 + rows_z, 4 - offset:4 - offset + rows_y]
        total = total + STENCIL_COEFS[offset] * (along_x + along_z + along_y)
    return total


def aperture_rows(anchor_tile):
    rows = anchor_tile.astype(jnp.int32) * TX + jnp.arange(AX, dtype=jnp.int32)
    return (rows % MX).astype(jnp.int32)


def reference(velocity, anchors, source_cells, receiver_cells, wavelet, residuals, forward_pair, adjoint_pair):
    def one_shot(items):
        anchor_tile, source, receivers, amplitude, residual, forward, adjoint = items
        local_velocity = jnp.take(velocity, aperture_rows(anchor_tile), axis=0)
        courant = (SPACING_RATIO * local_velocity) ** 2
        later_p, now_p = forward[0], forward[1]
        later_q, now_q = adjoint[0], adjoint[1]
        image = jnp.zeros_like(now_p)
        for step_index in range(STEPS):
            both = jnp.stack([now_p, now_q])
            padded = jnp.pad(both, ((0, 0), (4, 4), (4, 4), (4, 4)))
            laplace = stencil(padded, both)
            prev_p = 2.0 * now_p - later_p + courant * laplace[0]
            prev_p = prev_p.at[source[0], source[1], source[2]].add(amplitude[step_index])
            prev_q = 2.0 * now_q - later_q + courant * laplace[1]
            prev_q = prev_q.at[receivers[0], receivers[1], receivers[2]].add(residual[step_index])
            image = image + now_q * (later_p - 2.0 * now_p + prev_p)
            later_p, now_p = now_p, prev_p
            later_q, now_q = now_q, prev_q
        return jnp.stack([later_p, now_p]), jnp.stack([later_q, now_q]), image

    forward_out, adjoint_out, images = lax.map(one_shot, (anchors, source_cells, receiver_cells, wavelet, residuals, forward_pair, adjoint_pair))

    def place(shot_index, summed):
        return summed.at[aperture_rows(anchors[shot_index])].add(images[shot_index])

    summed = lax.fori_loop(0, N_SHOT, place, jnp.zeros(velocity.shape, jnp.float32))
    gradient = -(2.0 / velocity) * summed
    return gradient, forward_out, adjoint_out
```

```python
import functools

import jax
import jax.numpy as jnp
from jax import lax
from jax.experimental import pallas as pl
from jax.experimental.pallas import tpu as pltpu
from jax.sharding import PartitionSpec as P

APT = 4
RIM = 4
STENCIL_COEFS = (-205.0 / 72.0, 8.0 / 5.0, -1.0 / 5.0, 8.0 / 315.0, -1.0 / 560.0)
SPACING_RATIO = 0.1

F32 = jnp.float32
BF16 = jnp.bfloat16
IN_VMEM = pl.BlockSpec(memory_space=pltpu.VMEM)
IN_SMEM = pl.BlockSpec(memory_space=pltpu.SMEM)
IN_PLACE = pl.BlockSpec(memory_space=pl.ANY)


def kept(shape):
    return pltpu.VMEM(shape, F32)


def given(shape):
    return jax.ShapeDtypeStruct(shape, F32)


def on_chip(value):
    return pltpu.with_memory_space_constraint(value, pltpu.VMEM)


def call(kernel, outs, ins, out_specs=None, scratch=(), name=None):
    return pl.pallas_call(
        kernel,
        out_shape=tuple(outs),
        in_specs=[spec for spec, _ in ins],
        out_specs=tuple(out_specs or [IN_VMEM] * len(outs)),
        scratch_shapes=list(scratch),
        compiler_params=pltpu.CompilerParams(vmem_limit_bytes=40 * 1024 * 1024),
        name=name,
    )(*[array for _, array in ins])


def partners(count):
    reach = APT - 1
    if count <= 2 * reach and count & (count - 1) == 0:
        plans = []
        for bit in range(1, count):
            pairs = [(i, i ^ bit) for i in range(count)]
            plans.append((pairs, pairs, functools.partial(lambda bit, i: i ^ bit, bit)))
        return plans
    if count <= 2 * reach:
        offsets = range(1, count)
    else:
        offsets = [o for o in range(-reach, reach + 1) if o != 0]
    plans = []
    for o in offsets:
        fetch = [((i + o) % count, i) for i in range(count)]
        send = [(i, (i + o) % count) for i in range(count)]
        plans.append((fetch, send, functools.partial(lambda o, i: lax.rem(i + o + count, count), o)))
    return plans


def y_operator(width):
    row = lax.broadcasted_iota(jnp.int32, (width, width), 0)
    column = lax.broadcasted_iota(jnp.int32, (width, width), 1)
    apart = jnp.abs(row - column)
    total = jnp.zeros((width, width), F32)
    for o in range(1, RIM + 1):
        total = jnp.where(apart == o, F32(STENCIL_COEFS[o]), total)
    high = total.astype(BF16)
    return high, (total - high.astype(F32)).astype(BF16)


def y_part(field, high, low):
    rows, depth, width = field.shape
    flat = field.reshape(rows * depth, width)
    top = flat.astype(BF16)
    rest = (flat - top.astype(F32)).astype(BF16)
    total = jnp.dot(top, high, preferred_element_type=F32)
    total = total + jnp.dot(rest, high, preferred_element_type=F32)
    total = total + jnp.dot(top, low, preferred_element_type=F32)
    return total.reshape(rows, depth, width)


def xz_part(padded, rim, x, own, depth):
    total = F32(3.0 * STENCIL_COEFS[0]) * own
    window = jnp.concatenate([own, rim], axis=0)
    rows = depth + 2 * RIM
    for o in range(1, RIM + 1):
        pair = padded[x + RIM + o] + padded[x + RIM - o]
        below = pltpu.roll(window, rows - o, 0)[:depth]
        above = pltpu.roll(window, o, 0)[:depth]
        total = total + F32(STENCIL_COEFS[o]) * (pair + (below + above))
    return total


def fill_padded(padded, field):
    rows = padded.shape[0] - 2 * RIM
    zero = jnp.zeros((RIM,) + padded.shape[1:], F32)
    padded[0:RIM] = zero
    padded[RIM + rows : RIM + rows + RIM] = zero
    padded[RIM : RIM + rows] = field


def first_four(shape):
    return lax.broadcasted_iota(jnp.int32, shape, len(shape) - 2) < RIM


def pack_rims(p, q, depth):
    last = depth - 2 * RIM
    p_first, p_last = p[:, 0 : 2 * RIM], p[:, last:depth]
    q_first, q_last = q[:, 0 : 2 * RIM], q[:, last:depth]
    here = first_four(p_first.shape)
    deeper = jnp.where(here, pltpu.roll(q_last, RIM, 1), p_last)
    shallower = jnp.where(here, p_first, pltpu.roll(q_first, RIM, 1))
    return deeper, shallower


def p_rim(from_above, from_below):
    return jnp.where(first_four(from_above.shape), from_below, from_above)


def q_rim(from_above, from_below):
    both = jnp.where(first_four(from_above.shape), from_above, from_below)
    return pltpu.roll(both, RIM, both.ndim - 2)


def cell_mask(source, depth, width):
    start = lax.axis_index("sub") * depth
    layer = lax.broadcasted_iota(jnp.int32, (depth, width), 0)
    column = lax.broadcasted_iota(jnp.int32, (depth, width), 1)
    return (layer == source[0, 1] - start) & (column == source[0, 2])


def rims_kernel(p_ref, q_ref, deeper, shallower):
    depth = p_ref.shape[1]
    deeper[...], shallower[...] = pack_rims(p_ref[...], q_ref[...], depth)


def first_kernel(
    source, wavelet, receivers, residuals, forward, adjoint, above, below,
    free_p, lap_p, free_q, lap_q, mixed, free_q2, injected, padded, spread,
):
    rows, depth, width = lap_p.shape
    high, low = y_operator(width)
    start = lax.axis_index("sub") * depth

    first, layer, column = receivers[0, 0:1], receivers[0, 1:2] - start, receivers[0, 2:3]
    inside = (layer >= 0) & (layer < depth)
    place = jnp.where(inside, first * depth + layer, -1)
    count = place.shape[1]
    lines = lax.broadcasted_iota(jnp.int32, (rows * depth, count), 0)
    onto = (lines == place).astype(F32).astype(BF16)
    columns = lax.broadcasted_iota(jnp.int32, (width, count), 0)
    for step in range(2):
        value = jnp.where(columns == column, residuals[0, step : step + 1], 0.0)
        total = None
        for _ in range(3):
            part = value.astype(BF16)
            value = value - part.astype(F32)
            term = lax.dot_general(onto, part, (((1,), (1,)), ((), ())), preferred_element_type=F32)
            total = term if total is None else total + term
        spread[step] = total.reshape(rows, depth, width)

    here = cell_mask(source, depth, width)
    for name, pair, rim_of, lap, free in (
        ("p", forward, p_rim, lap_p, free_p), ("q", adjoint, q_rim, lap_q, free_q),
    ):
        fill_padded(padded, pair[0, 1])
        lap[...] = y_part(pair[0, 1], high, low)

        def row(x, _):
            own = pair[0, 1, x]
            rim = rim_of(above[x], below[x])
            value = lap[x] + xz_part(padded, rim, x, own, depth)
            lap[x] = value
            moved = 2.0 * own - pair[0, 0, x]
            if name == "q":
                moved = moved + spread[0, x]
                free_q2[x] = spread[1, x] - own
                mixed[x] = own * lap_p[x]
            free[x] = moved
            return 0

        lax.fori_loop(0, rows, row, 0, unroll=2)
    x0 = source[0, 0]
    amount = jnp.where(here, wavelet[0, 0], 0.0)
    free_p[x0] = free_p[x0] + amount
    injected[...] = adjoint[0, 1, x0] * amount


def step_kernel(plans, anchors, free_p, lap_p, free_q, lap_q, *refs):
    tiles, (courant, p1, q1, deeper, shallower) = refs[: len(plans) + 1], refs[len(plans) + 1 :]
    tile_rows = tiles[0].shape[0]
    depth = p1.shape[1]
    for tile, place in zip(tiles, places(plans, anchors)):

        def put():
            speed = F32(SPACING_RATIO) * tile[...]
            factor = speed * speed
            span = pl.ds(place * tile_rows, tile_rows)
            courant[span] = factor
            p = free_p[span] + factor * lap_p[span]
            q = free_q[span] + factor * lap_q[span]
            p1[span] = p
            q1[span] = q
            deeper[span], shallower[span] = pack_rims(p, q, depth)

        pl.when((place >= 0) & (place < APT))(put)


def places(plans, anchors):
    count = lax.axis_size("shot")
    me = lax.axis_index("shot")
    peers = [me] + [peer(me) for _, _, peer in plans]
    return [lax.rem(peer - anchors[0] + count, count) for peer in peers]


def image_kernel(plans, source, wavelet, anchors, p1, q1, courant, mixed, injected, above, below, *refs):
    outs, (lap_p, padded, image) = refs[: len(plans) + 1], refs[len(plans) + 1 :]
    rows, depth, width = p1.shape
    high, low = y_operator(width)
    fill_padded(padded, p1[...])
    lap_p[...] = y_part(p1[...], high, low)

    def row(x, _):
        own = p1[x]
        value = lap_p[x] + xz_part(padded, p_rim(above[x], below[x]), x, own, depth)
        lap_p[x] = value
        image[x] = courant[x] * (mixed[x] + q1[x] * value)
        return 0

    lax.fori_loop(0, rows, row, 0, unroll=2)
    x0 = source[0, 0]
    amount = jnp.where(cell_mask(source, depth, width), wavelet[0, 1], 0.0)
    image[x0] = image[x0] + injected[...] + q1[x0] * amount
    tile_rows = outs[0].shape[0]
    for out, place in zip(outs, places(plans, anchors)):
        inside = (place >= 0) & (place < APT)

        def put():
            out[...] = image[pl.ds(place * tile_rows, tile_rows)]

        def clear():
            out[...] = jnp.zeros(out.shape, F32)

        pl.when(inside)(put)
        pl.when(jnp.logical_not(inside))(clear)


def last_kernel(source, wavelet, forward, p1, q1, courant, lap_p, free_q2, above, below, forward_out, adjoint_out, padded):
    rows, depth, width = p1.shape
    high, low = y_operator(width)
    fill_padded(padded, q1[...])
    adjoint_out[0, 1] = y_part(q1[...], high, low)

    def row(x, _):
        own_p, own_q, factor = p1[x], q1[x], courant[x]
        forward_out[0, 0, x] = own_p
        adjoint_out[0, 0, x] = own_q
        forward_out[0, 1, x] = 2.0 * own_p - forward[x] + factor * lap_p[x]
        value = adjoint_out[0, 1, x] + xz_part(padded, q_rim(above[x], below[x]), x, own_q, depth)
        adjoint_out[0, 1, x] = 2.0 * own_q + free_q2[x] + factor * value
        return 0

    lax.fori_loop(0, rows, row, 0, unroll=2)
    x0 = source[0, 0]
    amount = jnp.where(cell_mask(source, depth, width), wavelet[0, 1], 0.0)
    forward_out[0, 1, x0] = forward_out[0, 1, x0] + amount


def gradient_kernel(velocity, *refs):
    parts, out = refs[:-1], refs[-1]
    total = parts[0][...]
    for part in parts[1:]:
        total = total + part[...]
    out[...] = -(2.0 / velocity[...]) * total


def swap_rims(deeper, shallower):
    count = lax.axis_size("sub")
    down = [(i, i + 1) for i in range(count - 1)]
    up = [(i + 1, i) for i in range(count - 1)]
    return lax.ppermute(deeper, "sub", down), lax.ppermute(shallower, "sub", up)


def on_device(
    velocity, anchors, source_cells, receiver_cells, wavelet, residuals, forward_pair, adjoint_pair
):
    tile_rows, depth, width = velocity.shape
    rows = APT * tile_rows
    field = (rows, depth, width)
    rim = (rows, 2 * RIM, width)
    padded = pltpu.VMEM((rows + 2 * RIM, depth, width), F32)
    plans = partners(lax.axis_size("shot"))

    tiles = [velocity] + [lax.ppermute(velocity, "shot", fetch) for fetch, _, _ in plans]

    now = pl.BlockSpec((None, None, rows, depth, width), lambda i: (0, 1, 0, 0, 0))
    whole_rim = pl.BlockSpec(rim, lambda i: (0, 0, 0))
    deeper, shallower = pl.pallas_call(
        rims_kernel, out_shape=(given(rim),) * 2, grid=(1,), in_specs=[now, now], out_specs=(whole_rim,) * 2,
        name="rims",
    )(forward_pair, adjoint_pair)
    above, below = swap_rims(deeper, shallower)

    free_p, lap_p, free_q, lap_q, mixed, free_q2, injected = call(
        first_kernel,
        [kept(field)] * 6 + [kept((depth, width))],
        [
            (IN_SMEM, source_cells), (IN_SMEM, wavelet), (IN_VMEM, receiver_cells), (IN_VMEM, residuals),
            (IN_VMEM, forward_pair), (IN_VMEM, adjoint_pair), (IN_VMEM, above), (IN_VMEM, below),
        ],
        scratch=[padded, pltpu.VMEM((2,) + field, F32)],
        name="first",
    )

    courant, p1, q1, deeper, shallower = call(
        functools.partial(step_kernel, plans),
        [kept(field)] * 3 + [given(rim)] * 2,
        [(IN_SMEM, anchors)]
        + [(IN_VMEM, on_chip(a)) for a in (free_p, lap_p, free_q, lap_q)]
        + [(IN_VMEM, tile) for tile in tiles],
        name="step",
    )
    above, below = swap_rims(deeper, shallower)

    *images, lap_p1 = call(
        functools.partial(image_kernel, plans),
        [given(velocity.shape)] * len(tiles) + [kept(field)],
        [(IN_SMEM, source_cells), (IN_SMEM, wavelet), (IN_SMEM, anchors)]
        + [(IN_VMEM, on_chip(a)) for a in (p1, q1, courant, mixed, injected)]
        + [(IN_VMEM, above), (IN_VMEM, below)],
        scratch=[padded, pltpu.VMEM(field, F32)],
        name="image",
    )
    gathered = [images[0]] + [
        lax.ppermute(image, "shot", send) for image, (_, send, _) in zip(images[1:], plans)
    ]

    forward_out, adjoint_out = call(
        last_kernel,
        [given(forward_pair.shape), given(adjoint_pair.shape)],
        [(IN_SMEM, source_cells), (IN_SMEM, wavelet), (IN_VMEM, forward_pair[0, 1])]
        + [(IN_VMEM, on_chip(a)) for a in (p1, q1, courant, lap_p1, free_q2)]
        + [(IN_VMEM, above), (IN_VMEM, below)],
        scratch=[padded],
        name="last",
    )

    (gradient,) = call(
        gradient_kernel,
        [given(velocity.shape)],
        [(IN_VMEM, velocity)] + [(IN_VMEM, part) for part in gathered],
        name="gradient",
    )
    return gradient, forward_out, adjoint_out


def solution(mesh):
    shot = ("grp", "shot")
    fields = P(shot, None, None, "sub", None)
    return jax.shard_map(
        on_device,
        mesh=mesh,
        in_specs=(
            P(shot, "sub", None),
            P(shot),
            P(shot, None),
            P(shot, None, None),
            P(shot, None),
            P(shot, None, None),
            fields,
            fields,
        ),
        out_specs=(P(shot, "sub", None), fields, fields),
        check_vma=False,
    )
```

```python
import functools

import jax
import jax.numpy as jnp
from jax import lax
from jax.experimental import pallas as pl
from jax.experimental.pallas import tpu as pltpu
from jax.sharding import PartitionSpec as P

APT = 4
RIM = 4
STENCIL_COEFS = (-205.0 / 72.0, 8.0 / 5.0, -1.0 / 5.0, 8.0 / 315.0, -1.0 / 560.0)
SPACING_RATIO = 0.1

F32 = jnp.float32
BF16 = jnp.bfloat16
IN_VMEM = pl.BlockSpec(memory_space=pltpu.VMEM)
IN_SMEM = pl.BlockSpec(memory_space=pltpu.SMEM)
LONG = pl.CostEstimate(flops=10**9, bytes_accessed=10**8, transcendentals=0)


def kept(shape):
    return pltpu.VMEM(shape, F32)


def given(shape):
    return jax.ShapeDtypeStruct(shape, F32)


def on_chip(value):
    return pltpu.with_memory_space_constraint(value, pltpu.VMEM)


def call(kernel, outs, ins, out_specs=None, scratch=(), name=None, long=False):
    return pl.pallas_call(
        kernel,
        out_shape=tuple(outs),
        in_specs=[spec for spec, _ in ins],
        out_specs=tuple(out_specs or [IN_VMEM] * len(outs)),
        scratch_shapes=list(scratch),
        compiler_params=pltpu.CompilerParams(vmem_limit_bytes=40 * 1024 * 1024),
        cost_estimate=LONG if long else None,
        name=name,
    )(*[array for _, array in ins])


def partners(count):
    reach = APT - 1
    if count <= 2 * reach and count & (count - 1) == 0:
        plans = []
        for bit in range(1, count):
            pairs = [(i, i ^ bit) for i in range(count)]
            plans.append((pairs, pairs, functools.partial(lambda bit, i: i ^ bit, bit)))
        return plans
    if count <= 2 * reach:
        offsets = range(1, count)
    else:
        offsets = [o for o in range(-reach, reach + 1) if o != 0]
    plans = []
    for o in offsets:
        fetch = [((i + o) % count, i) for i in range(count)]
        send = [(i, (i + o) % count) for i in range(count)]
        plans.append((fetch, send, functools.partial(lambda o, i: lax.rem(i + o + count, count), o)))
    return plans


def y_operator(width):
    row = lax.broadcasted_iota(jnp.int32, (width, width), 0)
    column = lax.broadcasted_iota(jnp.int32, (width, width), 1)
    apart = jnp.abs(row - column)
    total = jnp.zeros((width, width), F32)
    for o in range(1, RIM + 1):
        total = jnp.where(apart == o, F32(STENCIL_COEFS[o]), total)
    high = total.astype(BF16)
    return high, (total - high.astype(F32)).astype(BF16)


def y_part(field, high, low):
    rows, depth, width = field.shape
    flat = field.reshape(rows * depth, width)
    top = flat.astype(BF16)
    rest = (flat - top.astype(F32)).astype(BF16)
    total = jnp.dot(top, high, preferred_element_type=F32)
    total = total + jnp.dot(rest, high, preferred_element_type=F32)
    total = total + jnp.dot(top, low, preferred_element_type=F32)
    return total.reshape(rows, depth, width)


def xz_part(padded, x, own, depth):
    total = F32(3.0 * STENCIL_COEFS[0]) * own
    window = jnp.concatenate([own, jnp.zeros((2 * RIM,) + own.shape[1:], F32)], axis=0)
    rows = depth + 2 * RIM
    for o in range(1, RIM + 1):
        pair = padded[x + RIM + o] + padded[x + RIM - o]
        below = pltpu.roll(window, rows - o, 0)[:depth]
        above = pltpu.roll(window, o, 0)[:depth]
        total = total + F32(STENCIL_COEFS[o]) * (pair + (below + above))
    return total


def rim_part(rim):
    axis, size = rim.ndim - 2, 2 * RIM
    line = lax.broadcasted_iota(jnp.int32, rim.shape, axis)
    first, last = jnp.zeros(rim.shape, F32), jnp.zeros(rim.shape, F32)
    for o in range(1, RIM + 1):
        coef = F32(STENCIL_COEFS[o])
        first = first + jnp.where(line < o, coef, 0.0) * pltpu.roll(rim, o, axis)
        last = last + jnp.where(line >= size - o, coef, 0.0) * pltpu.roll(rim, size - o, axis)
    return first, last


def fill_padded(padded, field):
    rows = padded.shape[0] - 2 * RIM
    zero = jnp.zeros((RIM,) + padded.shape[1:], F32)
    padded[0:RIM] = zero
    padded[RIM + rows : RIM + rows + RIM] = zero
    padded[RIM : RIM + rows] = field


def first_four(shape):
    return lax.broadcasted_iota(jnp.int32, shape, len(shape) - 2) < RIM


def is_even():
    return lax.rem(lax.axis_index("sub"), 2) == 0


def pack_rims(field):
    rows, depth, _ = field.shape
    half = rows // 2
    first, last = field[:, 0 : 2 * RIM], field[:, depth - 2 * RIM : depth]
    here = first_four(first[:half].shape)
    deeper = jnp.where(here, pltpu.roll(last[:half], RIM, 1), last[half:])
    shallower = jnp.where(here, first[:half], pltpu.roll(first[half:], RIM, 1))
    even = is_even()
    return jnp.where(even, deeper, shallower), jnp.where(even, shallower, deeper)


def unpack_rims(pair, other):
    even = is_even()
    above, below = jnp.where(even, other, pair), jnp.where(even, pair, other)
    here = first_four(above.shape)
    low = jnp.where(here, below, pltpu.roll(above, RIM, 1))
    high = jnp.where(here, pltpu.roll(below, RIM, 1), above)
    return low, high


def add_rims(pair, other, add):
    half = pair.shape[0]
    for index, rim in enumerate(unpack_rims(pair[...], other[...])):
        add(slice(index * half, (index + 1) * half), *rim_part(rim))


def cell_mask(source, depth, width):
    start = lax.axis_index("sub") * depth
    layer = lax.broadcasted_iota(jnp.int32, (depth, width), 0)
    column = lax.broadcasted_iota(jnp.int32, (depth, width), 1)
    return (layer == source[0, 1] - start) & (column == source[0, 2])


def rims_kernel(p_ref, q_ref, pair, other):
    half = pair.shape[0] // 2
    for index, ref in enumerate((p_ref, q_ref)):
        span = slice(index * half, (index + 1) * half)
        pair[span], other[span] = pack_rims(ref[...])


def first_kernel(
    source, wavelet, receivers, residuals, forward, adjoint,
    free_p, lap_p, free_q, lap_q, free_q2, injected, padded, spread,
):
    rows, depth, width = lap_p.shape
    high, low = y_operator(width)
    start = lax.axis_index("sub") * depth

    first, layer, column = receivers[0, 0:1], receivers[0, 1:2] - start, receivers[0, 2:3]
    inside = (layer >= 0) & (layer < depth)
    place = jnp.where(inside, first * depth + layer, -1)
    count = place.shape[1]
    lines = lax.broadcasted_iota(jnp.int32, (rows * depth, count), 0)
    onto = (lines == place).astype(F32).astype(BF16)
    columns = lax.broadcasted_iota(jnp.int32, (width, count), 0)
    for step in range(2):
        value = jnp.where(columns == column, residuals[0, step : step + 1], 0.0)
        total = None
        for _ in range(3):
            part = value.astype(BF16)
            value = value - part.astype(F32)
            term = lax.dot_general(onto, part, (((1,), (1,)), ((), ())), preferred_element_type=F32)
            total = term if total is None else total + term
        spread[step] = total.reshape(rows, depth, width)

    here = cell_mask(source, depth, width)
    for name, pair, lap, free in (("p", forward, lap_p, free_p), ("q", adjoint, lap_q, free_q)):
        fill_padded(padded, pair[0, 1])
        lap[...] = y_part(pair[0, 1], high, low)

        def row(x, _):
            own = pair[0, 1, x]
            lap[x] = lap[x] + xz_part(padded, x, own, depth)
            moved = 2.0 * own - pair[0, 0, x]
            if name == "q":
                moved = moved + spread[0, x]
                free_q2[x] = spread[1, x] - own
            free[x] = moved
            return 0

        lax.fori_loop(0, rows, row, 0, unroll=2)
    x0 = source[0, 0]
    amount = jnp.where(here, wavelet[0, 0], 0.0)
    free_p[x0] = free_p[x0] + amount
    injected[...] = adjoint[0, 1, x0] * amount


def add_rims_to(full, pair, other):
    edge = full.shape[1] - 2 * RIM

    def add(span, first, last):
        full[span, 0 : 2 * RIM] = full[span, 0 : 2 * RIM] + first
        full[span, edge:] = full[span, edge:] + last

    add_rims(pair, other, add)


def full_kernel(lap_p, lap_q, pair, other, now_q, full_p, full_q, mixed):
    half = pair.shape[0] // 2
    for index, (lap, full) in enumerate(((lap_p, full_p), (lap_q, full_q))):
        full[...] = lap[...]
        part = slice(index * half, (index + 1) * half)
        add_rims_to(full, pair.at[part], other.at[part])
    mixed[...] = now_q[...] * full_p[...]


def step_kernel(plans, anchors, free_p, free_q, full_p, full_q, *refs):
    tiles, (courant, p1, q1, pair_p, other_p) = refs[: len(plans) + 1], refs[len(plans) + 1 :]
    tile_rows = tiles[0].shape[0]
    for tile, place in zip(tiles, places(plans, anchors)):

        def put():
            speed = F32(SPACING_RATIO) * tile[...]
            factor = speed * speed
            span = pl.ds(place * tile_rows, tile_rows)
            courant[span] = factor
            p1[span] = free_p[span] + factor * full_p[span]
            q1[span] = free_q[span] + factor * full_q[span]

        pl.when((place >= 0) & (place < APT))(put)
    pair_p[...], other_p[...] = pack_rims(p1[...])


def places(plans, anchors):
    count = lax.axis_size("shot")
    me = lax.axis_index("shot")
    peers = [me] + [peer(me) for _, _, peer in plans]
    return [lax.rem(peer - anchors[0] + count, count) for peer in peers]


def inner_kernel(source, wavelet, p1, q1, courant, mixed, injected, lap_p, image, padded):
    rows, depth, width = p1.shape
    high, low = y_operator(width)
    fill_padded(padded, p1[...])
    lap_p[...] = y_part(p1[...], high, low)

    def row(x, _):
        value = lap_p[x] + xz_part(padded, x, p1[x], depth)
        lap_p[x] = value
        image[x] = courant[x] * (mixed[x] + q1[x] * value)
        return 0

    lax.fori_loop(0, rows, row, 0, unroll=2)
    x0 = source[0, 0]
    amount = jnp.where(cell_mask(source, depth, width), wavelet[0, 1], 0.0)
    image[x0] = image[x0] + injected[...] + q1[x0] * amount


def image_kernel(plans, anchors, q1, courant, lap_p, image, pair, other, *refs):
    outs, (full_p, whole) = refs[: len(plans) + 1], refs[len(plans) + 1 :]
    depth = q1.shape[1]
    edge = depth - 2 * RIM
    full_p[...] = lap_p[...]
    whole[...] = image[...]

    def add(span, first, last):
        for lines, more in ((slice(0, 2 * RIM), first), (slice(edge, depth), last)):
            full_p[span, lines] = full_p[span, lines] + more
            whole[span, lines] = whole[span, lines] + courant[span, lines] * (q1[span, lines] * more)

    add_rims(pair, other, add)
    tile_rows = outs[0].shape[0]
    for out, place in zip(outs, places(plans, anchors)):
        inside = (place >= 0) & (place < APT)

        def put():
            out[...] = whole[pl.ds(place * tile_rows, tile_rows)]

        def clear():
            out[...] = jnp.zeros(out.shape, F32)

        pl.when(inside)(put)
        pl.when(jnp.logical_not(inside))(clear)


def rims_q_kernel(q1, _, pair, other):
    pair[...], other[...] = pack_rims(q1[...])


def last_kernel(source, wavelet, forward, p1, q1, courant, lap_p, free_q2, forward_out, part_q, padded):
    rows, depth, width = p1.shape
    high, low = y_operator(width)
    fill_padded(padded, q1[...])
    part_q[...] = y_part(q1[...], high, low)

    def row(x, _):
        own_p, own_q, factor = p1[x], q1[x], courant[x]
        forward_out[0, 0, x] = own_p
        forward_out[0, 1, x] = 2.0 * own_p - forward[x] + factor * lap_p[x]
        value = part_q[x] + xz_part(padded, x, own_q, depth)
        part_q[x] = 2.0 * own_q + free_q2[x] + factor * value
        return 0

    lax.fori_loop(0, rows, row, 0, unroll=2)
    x0 = source[0, 0]
    amount = jnp.where(cell_mask(source, depth, width), wavelet[0, 1], 0.0)
    forward_out[0, 1, x0] = forward_out[0, 1, x0] + amount


def last_q_kernel(q1, courant, part_q, pair, other, adjoint_out):
    edge = q1.shape[1] - 2 * RIM
    adjoint_out[0, 0] = q1[...]
    adjoint_out[0, 1] = part_q[...]

    def add(span, first, last):
        for lines, more in ((slice(0, 2 * RIM), first), (slice(edge, None), last)):
            adjoint_out[0, 1, span, lines] = adjoint_out[0, 1, span, lines] + courant[span, lines] * more

    add_rims(pair, other, add)


def gradient_kernel(velocity, *refs):
    parts, out = refs[:-1], refs[-1]
    total = parts[0][...]
    for part in parts[1:]:
        total = total + part[...]
    out[...] = -(2.0 / velocity[...]) * total


def swap_rims(pair, other):
    count = lax.axis_size("sub")

    def both_ways(start):
        ahead = [(i, i + 1) for i in range(start, count - 1, 2)]
        return ahead + [(i, j) for j, i in ahead]

    return lax.ppermute(pair, "sub", both_ways(0)), lax.ppermute(other, "sub", both_ways(1))


def on_device(
    velocity, anchors, source_cells, receiver_cells, wavelet, residuals, forward_pair, adjoint_pair
):
    tile_rows, depth, width = velocity.shape
    rows = APT * tile_rows
    field = (rows, depth, width)
    rim = (rows // 2, 2 * RIM, width)
    padded = pltpu.VMEM((rows + 2 * RIM, depth, width), F32)
    plans = partners(lax.axis_size("shot"))

    tiles = [velocity] + [lax.ppermute(velocity, "shot", fetch) for fetch, _, _ in plans]

    now = pl.BlockSpec((None, None, rows, depth, width), lambda i: (0, 1, 0, 0, 0))
    two_rims = pl.BlockSpec((rows, 2 * RIM, width), lambda i: (0, 0, 0))
    pair, other = pl.pallas_call(
        rims_kernel, out_shape=(given((rows, 2 * RIM, width)),) * 2, grid=(1,), in_specs=[now, now],
        out_specs=(two_rims,) * 2, name="rims",
    )(forward_pair, adjoint_pair)
    pair, other = swap_rims(pair, other)

    free_p, lap_p, free_q, lap_q, free_q2, injected = call(
        first_kernel,
        [kept(field)] * 5 + [kept((depth, width))],
        [
            (IN_SMEM, source_cells), (IN_SMEM, wavelet), (IN_VMEM, receiver_cells), (IN_VMEM, residuals),
            (IN_VMEM, forward_pair), (IN_VMEM, adjoint_pair),
        ],
        scratch=[padded, pltpu.VMEM((2,) + field, F32)],
        name="first",
        long=True,
    )

    full_p, full_q, mixed = call(
        full_kernel,
        [kept(field)] * 3,
        [(IN_VMEM, on_chip(a)) for a in (lap_p, lap_q)]
        + [(IN_VMEM, pair), (IN_VMEM, other), (IN_VMEM, adjoint_pair[0, 1])],
        name="full",
    )
    courant, p1, q1, pair_p, other_p = call(
        functools.partial(step_kernel, plans),
        [kept(field)] * 3 + [given(rim)] * 2,
        [(IN_SMEM, anchors)]
        + [(IN_VMEM, on_chip(a)) for a in (free_p, free_q, full_p, full_q)]
        + [(IN_VMEM, tile) for tile in tiles],
        name="step",
    )
    pair_p, other_p = swap_rims(pair_p, other_p)

    lap_p1, image = call(
        inner_kernel,
        [kept(field)] * 2,
        [(IN_SMEM, source_cells), (IN_SMEM, wavelet)]
        + [(IN_VMEM, on_chip(a)) for a in (p1, q1, courant, mixed, injected)],
        scratch=[padded],
        name="inner",
    )
    *images, lap_p1 = call(
        functools.partial(image_kernel, plans),
        [given(velocity.shape)] * len(tiles) + [kept(field)],
        [(IN_SMEM, anchors)]
        + [(IN_VMEM, on_chip(a)) for a in (q1, courant, lap_p1, image)]
        + [(IN_VMEM, pair_p), (IN_VMEM, other_p)],
        scratch=[pltpu.VMEM(field, F32)],
        name="image",
    )
    gathered = [images[0]] + [
        lax.ppermute(image, "shot", send) for image, (_, send, _) in zip(images[1:], plans)
    ]

    pair_q, other_q = call(
        rims_q_kernel, [given(rim)] * 2, [(IN_VMEM, on_chip(a)) for a in (q1, lap_p1)], name="rims_q"
    )
    pair_q, other_q = swap_rims(pair_q, other_q)
    forward_out, part_q = call(
        last_kernel,
        [given(forward_pair.shape), kept(field)],
        [(IN_SMEM, source_cells), (IN_SMEM, wavelet), (IN_VMEM, forward_pair[0, 1])]
        + [(IN_VMEM, on_chip(a)) for a in (p1, q1, courant, lap_p1, free_q2)],
        scratch=[padded],
        name="last",
        long=True,
    )
    (adjoint_out,) = call(
        last_q_kernel,
        [given(adjoint_pair.shape)],
        [(IN_VMEM, on_chip(a)) for a in (q1, courant, part_q)] + [(IN_VMEM, pair_q), (IN_VMEM, other_q)],
        name="last_q",
    )

    (gradient,) = call(
        gradient_kernel,
        [given(velocity.shape)],
        [(IN_VMEM, velocity)] + [(IN_VMEM, part) for part in gathered],
        name="gradient",
    )
    return gradient, forward_out, adjoint_out


def solution(mesh):
    shot = ("grp", "shot")
    fields = P(shot, None, None, "sub", None)
    return jax.shard_map(
        on_device,
        mesh=mesh,
        in_specs=(
            P(shot, "sub", None),
            P(shot),
            P(shot, None),
            P(shot, None, None),
            P(shot, None),
            P(shot, None, None),
            fields,
            fields,
        ),
        out_specs=(P(shot, "sub", None), fields, fields),
        check_vma=False,
    )
```

```python
import functools

import jax
import jax.numpy as jnp
from jax import lax
from jax.experimental import pallas as pl
from jax.experimental.pallas import tpu as pltpu
from jax.sharding import PartitionSpec as P

APT = 4
RIM = 4
SPACING_RATIO = 0.1
SCALE = 5040
CENTRE = (-43008.0, -42.0)
COEFS = (0.0, 8064.0, -1008.0, 128.0, -9.0)

F32 = jnp.float32
BF16 = jnp.bfloat16
IN_VMEM = pl.BlockSpec(memory_space=pltpu.VMEM)
IN_SMEM = pl.BlockSpec(memory_space=pltpu.SMEM)
IN_PLACE = pl.BlockSpec(memory_space=pltpu.HBM)
LONG = pl.CostEstimate(flops=10**10, bytes_accessed=10**8, transcendentals=0)
LAST = LONG


def kept(shape):
    return pltpu.VMEM(shape, F32)


def given(shape):
    return jax.ShapeDtypeStruct(shape, F32)


def on_chip(value):
    return pltpu.with_memory_space_constraint(value, pltpu.VMEM)


def on_smem(value):
    return pltpu.with_memory_space_constraint(value, pltpu.SMEM)


def in_hbm(value):
    return pltpu.with_memory_space_constraint(value, pltpu.HBM)


def call(kernel, outs, ins, out_specs=None, scratch=(), name=None, cost=None, aliases=None):
    return pl.pallas_call(
        kernel,
        out_shape=tuple(outs),
        in_specs=[spec for spec, _ in ins],
        out_specs=tuple(out_specs or [IN_VMEM] * len(outs)),
        scratch_shapes=list(scratch),
        compiler_params=pltpu.CompilerParams(vmem_limit_bytes=40 * 1024 * 1024),
        cost_estimate=cost,
        input_output_aliases=aliases or {},
        name=name,
    )(*[array for _, array in ins])


def partners(count):
    reach = APT - 1
    if count <= 2 * reach and count & (count - 1) == 0:
        plans = []
        middle = count // 2
        for bit in [*range(middle, count), *range(1, middle)]:
            pairs = [(i, i ^ bit) for i in range(count)]
            plans.append((pairs, pairs, functools.partial(lambda bit, i: i ^ bit, bit)))
        return plans
    if count <= 2 * reach:
        offsets = range(1, count)
    else:
        offsets = [o for o in range(-reach, reach + 1) if o != 0]
    plans = []
    for o in offsets:
        fetch = [((i + o) % count, i) for i in range(count)]
        send = [(i, (i + o) % count) for i in range(count)]
        plans.append((fetch, send, functools.partial(lambda o, i: lax.rem(i + o + count, count), o)))
    return plans


def coefs_at(apart):
    total = jnp.zeros(apart.shape, F32)
    for o in range(1, RIM + 1):
        total = jnp.where(apart == o, F32(COEFS[o]), total)
    return total


def put_operators(along_y, along_xz, across, depth):
    width, size = along_y.shape[1], along_xz.shape[0]

    def grid(columns):
        row = lax.broadcasted_iota(jnp.int32, (size, columns), 0)
        column = lax.broadcasted_iota(jnp.int32, (size, columns), 1)
        return lax.div(row, depth), lax.rem(row, depth), lax.div(column, depth), lax.rem(column, depth)

    row = lax.broadcasted_iota(jnp.int32, (width, width), 0)
    column = lax.broadcasted_iota(jnp.int32, (width, width), 1)
    value = jnp.where(row == column, F32(CENTRE[1]), coefs_at(jnp.abs(row - column))).astype(BF16)
    along_y[0:width] = value
    along_y[width:] = value

    x, z, other_x, other_z = grid(size)
    same_x, same_z = x == other_x, z == other_z
    value = jnp.where(same_z, coefs_at(jnp.abs(x - other_x)), 0.0)
    value = value + jnp.where(same_x, coefs_at(jnp.abs(z - other_z)), 0.0)
    value = jnp.where(same_x & same_z, F32(CENTRE[0]), value).astype(BF16)
    along_xz[:, 0:size] = value
    along_xz[:, size:] = value

    rim = RIM * depth
    x, z, other_x, other_z = grid(rim)
    for index, first in enumerate((size // depth, -RIM)):
        value = jnp.where(z == other_z, coefs_at(jnp.abs(other_x + first - x)), 0.0).astype(BF16)
        across[index, :, 0:rim] = value
        across[index, :, rim:] = value


def put_laplacian(out, field, along_y, along_xz, across):
    rows, depth, width = field.shape
    flat = field.reshape(rows * depth, width)
    top = flat.astype(BF16)
    rest = (flat - top.astype(F32)).astype(BF16)
    size, rim = along_xz.shape[0], RIM * depth
    for start in range(0, rows * depth, size):
        here = slice(start, start + size)
        left = [top[here], rest[here], along_xz[...]]
        right = [along_y[...], top[here], rest[here]]
        sides = ((0, start + size), (1, start - rim))
        for index, low in sides:
            if 0 <= low < rows * depth:
                left.append(across[index])
                right += [top[low : low + rim], rest[low : low + rim]]
        total = jnp.dot(
            jnp.concatenate(left, axis=1), jnp.concatenate(right, axis=0), preferred_element_type=F32
        )
        out[start // depth : (start + size) // depth] = total.reshape(size // depth, depth, width)


def first_four(shape):
    return lax.broadcasted_iota(jnp.int32, shape, len(shape) - 2) < RIM


def is_even():
    return lax.rem(lax.axis_index("sub"), 2) == 0


def pack_rims(field):
    rows, depth, _ = field.shape
    half = rows // 2
    first, last = field[:, 0 : 2 * RIM], field[:, depth - 2 * RIM : depth]
    here = first_four(first[:half].shape)
    deeper = jnp.where(here, pltpu.roll(last[:half], RIM, 1), last[half:])
    shallower = jnp.where(here, first[:half], pltpu.roll(first[half:], RIM, 1))
    even = is_even()
    return jnp.where(even, deeper, shallower), jnp.where(even, shallower, deeper)


def side_part(message, below, index):
    axis, size = message.ndim - 2, 2 * RIM
    line = lax.broadcasted_iota(jnp.int32, message.shape, axis)
    turn = RIM * (index if below else 1 - index)
    total = None
    for o in range(1, RIM + 1):
        reached = line >= size - o if below else line < o
        shift = (turn + (size - o if below else o)) % size
        moved = pltpu.roll(message, shift, axis) if shift else message
        term = jnp.where(reached, F32(COEFS[o]), 0.0) * moved
        total = term if total is None else total + term
    return total


def add_side(message, pair, depth, add):
    half = message.shape[0]
    for even in (True, False):
        below = pair == even

        def put(below=below):
            layers = slice(depth - 2 * RIM, depth) if below else slice(0, 2 * RIM)
            for index in range(2):
                add(slice(index * half, (index + 1) * half), layers, side_part(message[...], below, index))

        pl.when(is_even() == even)(put)


def cell_mask(cells, depth, width):
    start = lax.axis_index("sub") * depth
    layer = lax.broadcasted_iota(jnp.int32, (depth, width), 0)
    column = lax.broadcasted_iota(jnp.int32, (depth, width), 1)
    return (layer == cells[1] - start) & (column == cells[2])


def load(sources, fields, sems):
    pieces = sems.shape[1]
    copies = []
    for index, (source, field) in enumerate(zip(sources, fields)):
        step = field.shape[0] // pieces
        for piece in range(pieces):
            span = pl.ds(piece * step, step)
            copies.append(pltpu.make_async_copy(source.at[span], field.at[span], sems.at[index, piece]))
    for copy in copies:
        copy.start()
    return copies


def rims_kernel(
    forward, adjoint, velocity, pair, other, p, q, *refs
):
    onto, (sems, small_sems) = refs[:-2], refs[-2:]
    half = pair.shape[0] // 2
    copies = load((forward.at[0, 1], adjoint.at[0, 1]), (p, q), sems)
    small = [
        pltpu.make_async_copy(source, target, small_sems.at[index])
        for index, (source, target) in enumerate(zip((velocity,), onto))
    ]
    for copy in small:
        copy.start()
    for index, field in enumerate((p, q)):
        for copy in copies[index * len(copies) // 2 : (index + 1) * len(copies) // 2]:
            copy.wait()
        span = slice(index * half, (index + 1) * half)
        pair[span], other[span] = pack_rims(field[...])
    for copy in small:
        copy.wait()


def first_kernel(
    source, wavelet, anchors, receivers_in, residuals_in, forward, adjoint, p, q,
    cells, amounts, free_p, lap_p, free_q, lap_q, free_q2, mixed, along_y, along_xz, across,
    spread, later, receivers, residuals, sems, small_sems,
):
    rows, depth, width = lap_p.shape
    for index in range(3):
        cells[index] = source[0, index]
    cells[3] = jnp.max(anchors[...])
    for step in range(2):
        amounts[step] = wavelet[0, step]
    copies = load((forward.at[0, 0], adjoint.at[0, 0]), (later.at[0], later.at[1]), sems)
    small = [
        pltpu.make_async_copy(given_ref, target, small_sems.at[index])
        for index, (given_ref, target) in enumerate(
            ((receivers_in, receivers), (residuals_in, residuals))
        )
    ]
    for copy in small:
        copy.start()
    put_operators(along_y, along_xz, across, depth)
    put_laplacian(lap_p, p[...], along_y, along_xz, across)
    put_laplacian(lap_q, q[...], along_y, along_xz, across)
    for copy in small:
        copy.wait()
    start = lax.axis_index("sub") * depth

    first, layer, column = receivers[0], receivers[1] - start, receivers[2]
    inside = (layer >= 0) & (layer < depth)
    place = jnp.where(inside, first * depth + layer, -1)
    count = place.shape[1]
    lines = lax.broadcasted_iota(jnp.int32, (rows * depth, count), 0)
    onto = (lines == place).astype(F32).astype(BF16)
    columns = lax.broadcasted_iota(jnp.int32, (width, count), 0)
    for step in range(2):
        value = jnp.where(columns == column, residuals[0, step : step + 1], 0.0)
        total = None
        for _ in range(3):
            part = value.astype(BF16)
            value = value - part.astype(F32)
            term = lax.dot_general(onto, part, (((1,), (1,)), ((), ())), preferred_element_type=F32)
            total = term if total is None else total + term
        spread[step] = total.reshape(rows, depth, width)

    for copy in copies:
        copy.wait()

    def row(x, _):
        own = q[x]
        free_p[x] = 2.0 * p[x] - later[0, x]
        free_q[x] = 2.0 * own - later[1, x] + spread[0, x]
        free_q2[x] = spread[1, x] - own
        mixed[x] = own * lap_p[x]
        return 0

    lax.fori_loop(0, rows, row, 0, unroll=4)


def full_kernel(lap_p, lap_q, mixed, now_q, pair, other, full_p, full_q, full_mixed):
    depth = lap_p.shape[1]
    half = pair.shape[0] // 2
    full_p[...] = lap_p[...]
    full_q[...] = lap_q[...]
    full_mixed[...] = mixed[...]

    def add_p(span, layers, part):
        full_p[span, layers] = full_p[span, layers] + part
        full_mixed[span, layers] = full_mixed[span, layers] + now_q[span, layers] * part

    def add_q(span, layers, part):
        full_q[span, layers] = full_q[span, layers] + part

    for message, is_pair in ((pair, True), (other, False)):
        add_side(message.at[0:half], is_pair, depth, add_p)
        add_side(message.at[half:], is_pair, depth, add_q)


def step_kernel(plans, cells, amounts, free_p, free_q, full_p, full_q, *refs):
    tiles, (courant, p1, q1, pair, other_p, other_q) = refs[: len(plans) + 1], refs[len(plans) + 1 :]
    tile_rows = tiles[0].shape[0]
    for tile, place in zip(tiles, places(plans, cells)):

        def put():
            speed = F32(SPACING_RATIO) * tile[...]
            factor = speed * speed * F32(1.0 / SCALE)
            span = pl.ds(place * tile_rows, tile_rows)
            courant[span] = factor
            p1[span] = free_p[span] + factor * full_p[span]
            q1[span] = free_q[span] + factor * full_q[span]

        pl.when((place >= 0) & (place < APT))(put)
    rows, depth, width = p1.shape
    half = rows // 2
    x0 = cells[0]
    p1[x0] = p1[x0] + jnp.where(cell_mask(cells, depth, width), amounts[0], 0.0)
    pair[0:half], other_p[...] = pack_rims(p1[...])
    pair[half:], other_q[...] = pack_rims(q1[...])


def places(plans, cells):
    count = lax.axis_size("shot")
    me = lax.axis_index("shot")
    peers = [me] + [peer(me) for _, _, peer in plans]
    return [lax.rem(peer - cells[3] + count, count) for peer in peers]


def put_tile(out, image, place):
    tile_rows = out.shape[0]
    inside = (place >= 0) & (place < APT)

    def put():
        out[...] = image[pl.ds(place * tile_rows, tile_rows)]

    def clear():
        out[...] = jnp.zeros(out.shape, F32)

    pl.when(inside)(put)
    pl.when(jnp.logical_not(inside))(clear)


def inner_kernel(p1, along_y, along_xz, across, lap_p):
    put_laplacian(lap_p, p1[...], along_y, along_xz, across)


def image_kernel(
    plans, cells, amounts, q0, q1, courant, mixed, lap_p, pair, other, full_p, *refs
):
    outs, image = refs[:-1], refs[-1]
    rows, depth, width = q1.shape
    full_p[...] = lap_p[...]

    def add(span, layers, part):
        full_p[span, layers] = full_p[span, layers] + part

    add_side(pair.at[0 : rows // 2], True, depth, add)
    add_side(other, False, depth, add)

    def row(x, _):
        image[x] = courant[x] * (mixed[x] + q1[x] * full_p[x])
        return 0

    lax.fori_loop(0, rows, row, 0, unroll=4)
    x0 = cells[0]
    here = cell_mask(cells, depth, width)
    added = q0[x0] * jnp.where(here, amounts[0], 0.0) + q1[x0] * jnp.where(here, amounts[1], 0.0)
    image[x0] = image[x0] + added
    for out, place in zip(outs, places(plans, cells)):
        put_tile(out, image, place)


def last_kernel(
    cells, amounts, p0, p1, q1, courant, lap_p, free_q2, along_y, along_xz, across, pair, other,
    forward_out, adjoint_out, p2, q2, lap_q, sems,
):
    rows, depth, width = p1.shape
    copies = []

    def save(field, out):
        copies.append(pltpu.make_async_copy(field, out, sems.at[len(copies)]))
        copies[-1].start()

    save(p1, forward_out.at[0, 0])
    save(q1, adjoint_out.at[0, 0])

    def row_p(x, _):
        p2[x] = 2.0 * p1[x] - p0[x] + courant[x] * lap_p[x]
        return 0

    lax.fori_loop(0, rows, row_p, 0, unroll=4)
    x0 = cells[0]
    amount = jnp.where(cell_mask(cells, depth, width), amounts[1], 0.0)
    p2[x0] = p2[x0] + amount
    save(p2, forward_out.at[0, 1])
    put_laplacian(lap_q, q1[...], along_y, along_xz, across)

    def add(span, layers, part):
        lap_q[span, layers] = lap_q[span, layers] + part

    add_side(pair.at[rows // 2 :], True, depth, add)
    add_side(other, False, depth, add)

    def row_q(x, _):
        q2[x] = 2.0 * q1[x] + free_q2[x] + courant[x] * lap_q[x]
        return 0

    lax.fori_loop(0, rows, row_q, 0, unroll=4)
    save(q2, adjoint_out.at[0, 1])
    for copy in copies:
        copy.wait()


def gradient_kernel(velocity, *refs):
    parts, out = refs[:-1], refs[-1]
    total = parts[0][...]
    for part in parts[1:]:
        total = total + part[...]
    out[...] = -(2.0 / velocity[...]) * total


def swap(message, start):
    ahead = [(i, i + 1) for i in range(start, lax.axis_size("sub") - 1, 2)]
    return lax.ppermute(message, "sub", ahead + [(i, j) for j, i in ahead])


def on_device(
    velocity, anchors, source_cells, receiver_cells, wavelet, residuals, forward_pair, adjoint_pair
):
    tile_rows, depth, width = velocity.shape
    rows = APT * tile_rows
    receiver_cells = jnp.transpose(receiver_cells, (1, 0, 2))
    field = (rows, depth, width)
    rims = (rows, 2 * RIM, width)
    plans = partners(lax.axis_size("shot"))
    plans_in = [plans[0], *plans[:0:-1]]

    arriving = [lax.ppermute(velocity, "shot", fetch) for fetch, _, _ in plans_in]

    pair, other, p0, q0, tile = call(
        rims_kernel,
        [given(rims)] * 2 + [kept(field)] * 2 + [kept(velocity.shape)],
        [(IN_PLACE, in_hbm(a)) for a in (forward_pair, adjoint_pair, velocity)],
        out_specs=[IN_VMEM] * 5,
        scratch=[pltpu.SemaphoreType.DMA((2, 4)), pltpu.SemaphoreType.DMA((1,))],
        name="rims",
    )
    pair, other = swap(pair, 0), swap(other, 1)

    size = min(rows, 256 // depth) * depth
    operators = [
        pltpu.VMEM((2 * width, width), BF16),
        pltpu.VMEM((size, 2 * size), BF16),
        pltpu.VMEM((2, size, 2 * RIM * depth), BF16),
    ]
    cells, amounts, free_p, lap_p, free_q, lap_q, free_q2, mixed, *operators = call(
        first_kernel,
        [pltpu.SMEM((4,), jnp.int32), pltpu.SMEM((2,), F32)] + [kept(field)] * 6 + operators,
        [
            (IN_SMEM, source_cells), (IN_SMEM, wavelet), (IN_VMEM, anchors),
            (IN_PLACE, in_hbm(receiver_cells)), (IN_PLACE, in_hbm(residuals)),
            (IN_PLACE, in_hbm(forward_pair)), (IN_PLACE, in_hbm(adjoint_pair)),
            (IN_VMEM, on_chip(p0)), (IN_VMEM, on_chip(q0)),
        ],
        out_specs=[IN_SMEM] * 2 + [IN_VMEM] * 9,
        scratch=[
            pltpu.VMEM((2,) + field, F32),
            pltpu.VMEM((2,) + field, F32),
            pltpu.VMEM(receiver_cells.shape, jnp.int32),
            pltpu.VMEM(residuals.shape, F32),
            pltpu.SemaphoreType.DMA((2, 2)),
            pltpu.SemaphoreType.DMA((2,)),
        ],
        name="first",
        cost=LONG,
    )
    scalars = [(IN_SMEM, on_smem(cells)), (IN_SMEM, on_smem(amounts))]

    full_p, full_q, mixed = call(
        full_kernel,
        [kept(field)] * 3,
        [(IN_VMEM, on_chip(a)) for a in (lap_p, lap_q, mixed, q0)] + [(IN_VMEM, pair), (IN_VMEM, other)],
        name="full",
    )
    courant, p1, q1, pair, other_p, other_q = call(
        functools.partial(step_kernel, plans_in),
        [kept(field)] * 3 + [given(rims)] + [given((rows // 2, 2 * RIM, width))] * 2,
        scalars
        + [(IN_VMEM, on_chip(a)) for a in (free_p, free_q, full_p, full_q)]
        + [(IN_VMEM, on_chip(tile))]
        + [(IN_VMEM, other_tile) for other_tile in arriving],
        name="step",
    )
    pair, other_p, other_q = swap(pair, 0), swap(other_p, 1), swap(other_q, 1)

    (lap_p1,) = call(
        inner_kernel,
        [kept(field)],
        [(IN_VMEM, on_chip(a)) for a in (p1, *operators)],
        name="inner",
    )
    lap_p1, *images = call(
        functools.partial(image_kernel, plans),
        [kept(field)] + [given(velocity.shape)] * (len(plans) + 1),
        scalars
        + [(IN_VMEM, on_chip(a)) for a in (q0, q1, courant, mixed, lap_p1)]
        + [(IN_VMEM, pair), (IN_VMEM, other_p)],
        scratch=[pltpu.VMEM(field, F32)],
        name="image",
    )
    gathered = [images[0]] + [
        lax.ppermute(image, "shot", send) for image, (_, send, _) in zip(images[1:], plans)
    ]

    forward_out, adjoint_out = call(
        last_kernel,
        [given(forward_pair.shape), given(adjoint_pair.shape)],
        scalars
        + [(IN_VMEM, on_chip(a)) for a in (p0, p1, q1, courant, lap_p1, free_q2, *operators)]
        + [(IN_VMEM, pair), (IN_VMEM, other_q)],
        out_specs=[IN_PLACE, IN_PLACE],
        scratch=[pltpu.VMEM(field, F32)] * 3 + [pltpu.SemaphoreType.DMA((4,))],
        name="last",
        cost=LAST,
    )

    (gradient,) = call(
        gradient_kernel,
        [given(velocity.shape)],
        [(IN_VMEM, a) for a in (on_chip(tile), *gathered)],
        name="gradient",
    )
    return gradient, forward_out, adjoint_out


def solution(mesh):
    shot = ("grp", "shot")
    fields = P(shot, None, None, "sub", None)
    return jax.shard_map(
        on_device,
        mesh=mesh,
        in_specs=(
            P(shot, "sub", None),
            P(shot),
            P(shot, None),
            P(shot, None, None),
            P(shot, None),
            P(shot, None, None),
            fields,
            fields,
        ),
        out_specs=(P(shot, "sub", None), fields, fields),
        check_vma=False,
    )
```

```python
import functools

import jax
import jax.numpy as jnp
from jax import lax
from jax.experimental import pallas as pl
from jax.experimental.pallas import tpu as pltpu
from jax.sharding import PartitionSpec as P

APT = 4
RIM = 4
SPACING_RATIO = 0.1
SCALE = 5040
CENTRE = (-43008.0, -42.0)
COEFS = (0.0, 8064.0, -1008.0, 128.0, -9.0)

F32 = jnp.float32
BF16 = jnp.bfloat16
IN_VMEM = pl.BlockSpec(memory_space=pltpu.VMEM)
IN_SMEM = pl.BlockSpec(memory_space=pltpu.SMEM)
IN_PLACE = pl.BlockSpec(memory_space=pltpu.HBM)
LONG = pl.CostEstimate(flops=10**10, bytes_accessed=10**8, transcendentals=0)


def kept(shape):
    return pltpu.VMEM(shape, F32)


def given(shape):
    return jax.ShapeDtypeStruct(shape, F32)


def on_chip(value):
    return pltpu.with_memory_space_constraint(value, pltpu.VMEM)


def on_smem(value):
    return pltpu.with_memory_space_constraint(value, pltpu.SMEM)


def in_hbm(value):
    return pltpu.with_memory_space_constraint(value, pltpu.HBM)


def call(kernel, outs, ins, out_specs=None, scratch=(), name=None, cost=None, aliases=None):
    return pl.pallas_call(
        kernel,
        out_shape=tuple(outs),
        in_specs=[spec for spec, _ in ins],
        out_specs=tuple(out_specs or [IN_VMEM] * len(outs)),
        scratch_shapes=list(scratch),
        compiler_params=pltpu.CompilerParams(vmem_limit_bytes=40 * 1024 * 1024),
        cost_estimate=cost,
        input_output_aliases=aliases or {},
        name=name,
    )(*[array for _, array in ins])


def partners(count):
    reach = APT - 1
    if count <= 2 * reach and count & (count - 1) == 0:
        plans = []
        middle = count // 2
        for bit in [*range(middle, count), *range(1, middle)]:
            pairs = [(i, i ^ bit) for i in range(count)]
            plans.append((pairs, pairs, functools.partial(lambda bit, i: i ^ bit, bit)))
        return plans
    if count <= 2 * reach:
        offsets = range(1, count)
    else:
        offsets = [o for o in range(-reach, reach + 1) if o != 0]
    plans = []
    for o in offsets:
        fetch = [((i + o) % count, i) for i in range(count)]
        send = [(i, (i + o) % count) for i in range(count)]
        plans.append((fetch, send, functools.partial(lambda o, i: lax.rem(i + o + count, count), o)))
    return plans


def coefs_at(apart):
    total = jnp.zeros(apart.shape, F32)
    for o in range(1, RIM + 1):
        total = jnp.where(apart == o, F32(COEFS[o]), total)
    return total


def put_operators(along_y, along_xz, across, depth):
    width, size = along_y.shape[1], along_xz.shape[0]

    def grid(columns):
        row = lax.broadcasted_iota(jnp.int32, (size, columns), 0)
        column = lax.broadcasted_iota(jnp.int32, (size, columns), 1)
        return lax.div(row, depth), lax.rem(row, depth), lax.div(column, depth), lax.rem(column, depth)

    row = lax.broadcasted_iota(jnp.int32, (width, width), 0)
    column = lax.broadcasted_iota(jnp.int32, (width, width), 1)
    value = jnp.where(row == column, F32(CENTRE[1]), coefs_at(jnp.abs(row - column))).astype(BF16)
    along_y[0:width] = value
    along_y[width:] = value

    x, z, other_x, other_z = grid(size)
    same_x, same_z = x == other_x, z == other_z
    value = jnp.where(same_z, coefs_at(jnp.abs(x - other_x)), 0.0)
    value = value + jnp.where(same_x, coefs_at(jnp.abs(z - other_z)), 0.0)
    value = jnp.where(same_x & same_z, F32(CENTRE[0]), value).astype(BF16)
    along_xz[:, 0:size] = value
    along_xz[:, size:] = value

    rim = RIM * depth
    x, z, other_x, other_z = grid(rim)
    for index, first in enumerate((size // depth, -RIM)):
        value = jnp.where(z == other_z, coefs_at(jnp.abs(other_x + first - x)), 0.0).astype(BF16)
        across[index, :, 0:rim] = value
        across[index, :, rim:] = value


def put_laplacian(out, field, along_y, along_xz, across):
    rows, depth, width = field.shape
    flat = field.reshape(rows * depth, width)
    top = flat.astype(BF16)
    rest = (flat - top.astype(F32)).astype(BF16)
    size, rim = along_xz.shape[0], RIM * depth
    for start in range(0, rows * depth, size):
        here = slice(start, start + size)
        left = [top[here], rest[here], along_xz[...]]
        right = [along_y[...], top[here], rest[here]]
        sides = ((0, start + size), (1, start - rim))
        for index, low in sides:
            if 0 <= low < rows * depth:
                left.append(across[index])
                right += [top[low : low + rim], rest[low : low + rim]]
        total = jnp.dot(
            jnp.concatenate(left, axis=1), jnp.concatenate(right, axis=0), preferred_element_type=F32
        )
        out[start // depth : (start + size) // depth] = total.reshape(size // depth, depth, width)


def first_four(shape):
    return lax.broadcasted_iota(jnp.int32, shape, len(shape) - 2) < RIM


def is_even():
    return lax.rem(lax.axis_index("sub"), 2) == 0


def pack_rims(field):
    rows, depth, _ = field.shape
    half = rows // 2
    first, last = field[:, 0 : 2 * RIM], field[:, depth - 2 * RIM : depth]
    here = first_four(first[:half].shape)
    deeper = jnp.where(here, pltpu.roll(last[:half], RIM, 1), last[half:])
    shallower = jnp.where(here, first[:half], pltpu.roll(first[half:], RIM, 1))
    even = is_even()
    return jnp.where(even, deeper, shallower), jnp.where(even, shallower, deeper)


def side_part(message, below, index):
    axis, size = message.ndim - 2, 2 * RIM
    line = lax.broadcasted_iota(jnp.int32, message.shape, axis)
    turn = RIM * (index if below else 1 - index)
    total = None
    for o in range(1, RIM + 1):
        reached = line >= size - o if below else line < o
        shift = (turn + (size - o if below else o)) % size
        moved = pltpu.roll(message, shift, axis) if shift else message
        term = jnp.where(reached, F32(COEFS[o]), 0.0) * moved
        total = term if total is None else total + term
    return total


def add_side(message, pair, depth, add):
    half = message.shape[0]
    for even in (True, False):
        below = pair == even

        def put(below=below):
            layers = slice(depth - 2 * RIM, depth) if below else slice(0, 2 * RIM)
            for index in range(2):
                add(slice(index * half, (index + 1) * half), layers, side_part(message[...], below, index))

        pl.when(is_even() == even)(put)


def cell_mask(cells, depth, width):
    start = lax.axis_index("sub") * depth
    layer = lax.broadcasted_iota(jnp.int32, (depth, width), 0)
    column = lax.broadcasted_iota(jnp.int32, (depth, width), 1)
    return (layer == cells[0, 1] - start) & (column == cells[0, 2])


def load(sources, fields, sems):
    pieces = sems.shape[1]
    copies = []
    for index, (source, field) in enumerate(zip(sources, fields)):
        step = field.shape[0] // pieces
        for piece in range(pieces):
            span = pl.ds(piece * step, step)
            copies.append(pltpu.make_async_copy(source.at[span], field.at[span], sems.at[index, piece]))
    for copy in copies:
        copy.start()
    return copies


def rims_kernel(
    forward, adjoint, velocity, source, wavelet, pair, other, p, q, *refs
):
    onto, (sems, small_sems) = refs[:-2], refs[-2:]
    half = pair.shape[0] // 2
    copies = load((forward.at[0, 1], adjoint.at[0, 1]), (p, q), sems)
    small = [
        pltpu.make_async_copy(source, target, small_sems.at[index])
        for index, (source, target) in enumerate(zip((velocity, source, wavelet), onto))
    ]
    for copy in small:
        copy.start()
    for index, field in enumerate((p, q)):
        for copy in copies[index * len(copies) // 2 : (index + 1) * len(copies) // 2]:
            copy.wait()
        span = slice(index * half, (index + 1) * half)
        pair[span], other[span] = pack_rims(field[...])
    for copy in small:
        copy.wait()


def first_kernel(
    receivers_in, residuals_in, forward, adjoint, p, q,
    free_p, lap_p, free_q, lap_q, free_q2, mixed, along_y, along_xz, across,
    spread, later, receivers, residuals, sems, small_sems,
):
    rows, depth, width = lap_p.shape
    copies = load((forward.at[0, 0], adjoint.at[0, 0]), (later.at[0], later.at[1]), sems)
    small = [
        pltpu.make_async_copy(given_ref, target, small_sems.at[index])
        for index, (given_ref, target) in enumerate(
            ((receivers_in, receivers), (residuals_in, residuals))
        )
    ]
    for copy in small:
        copy.start()
    put_operators(along_y, along_xz, across, depth)
    put_laplacian(lap_p, p[...], along_y, along_xz, across)
    put_laplacian(lap_q, q[...], along_y, along_xz, across)
    for copy in small:
        copy.wait()
    start = lax.axis_index("sub") * depth

    first, layer, column = receivers[0], receivers[1] - start, receivers[2]
    inside = (layer >= 0) & (layer < depth)
    place = jnp.where(inside, first * depth + layer, -1)
    count = place.shape[1]
    lines = lax.broadcasted_iota(jnp.int32, (rows * depth, count), 0)
    onto = (lines == place).astype(F32).astype(BF16)
    columns = lax.broadcasted_iota(jnp.int32, (width, count), 0)
    for step in range(2):
        value = jnp.where(columns == column, residuals[0, step : step + 1], 0.0)
        total = None
        for _ in range(3):
            part = value.astype(BF16)
            value = value - part.astype(F32)
            term = lax.dot_general(onto, part, (((1,), (1,)), ((), ())), preferred_element_type=F32)
            total = term if total is None else total + term
        spread[step] = total.reshape(rows, depth, width)

    for copy in copies:
        copy.wait()

    def row(x, _):
        own = q[x]
        free_p[x] = 2.0 * p[x] - later[0, x]
        free_q[x] = 2.0 * own - later[1, x] + spread[0, x]
        free_q2[x] = spread[1, x] - own
        mixed[x] = own * lap_p[x]
        return 0

    lax.fori_loop(0, rows, row, 0, unroll=4)


def full_kernel(lap_p, lap_q, mixed, now_q, other, pair, full_p, full_q, full_mixed):
    depth = lap_p.shape[1]
    half = pair.shape[0] // 2
    full_p[...] = lap_p[...]
    full_q[...] = lap_q[...]
    full_mixed[...] = mixed[...]

    def add_p(span, layers, part):
        full_p[span, layers] = full_p[span, layers] + part
        full_mixed[span, layers] = full_mixed[span, layers] + now_q[span, layers] * part

    def add_q(span, layers, part):
        full_q[span, layers] = full_q[span, layers] + part

    for message, is_pair in ((pair, True), (other, False)):
        add_side(message.at[0:half], is_pair, depth, add_p)
        add_side(message.at[half:], is_pair, depth, add_q)


def step_kernel(plans, anchors, cells, amounts, free_p, free_q, full_p, full_q, *refs):
    tiles, (courant, p1, q1, pair, other_p, other_q) = refs[: len(plans) + 1], refs[len(plans) + 1 :]
    tile_rows = tiles[0].shape[0]
    for tile, place in zip(tiles, places(plans, anchors)):

        def put():
            speed = F32(SPACING_RATIO) * tile[...]
            factor = speed * speed * F32(1.0 / SCALE)
            span = pl.ds(place * tile_rows, tile_rows)
            courant[span] = factor
            p1[span] = free_p[span] + factor * full_p[span]
            q1[span] = free_q[span] + factor * full_q[span]

        pl.when((place >= 0) & (place < APT))(put)
    rows, depth, width = p1.shape
    half = rows // 2
    x0 = cells[0, 0]
    p1[x0] = p1[x0] + jnp.where(cell_mask(cells, depth, width), amounts[0, 0], 0.0)
    pair[0:half], other_p[...] = pack_rims(p1[...])
    pair[half:], other_q[...] = pack_rims(q1[...])


def places(plans, anchors):
    count = lax.axis_size("shot")
    me = lax.axis_index("shot")
    peers = [me] + [peer(me) for _, _, peer in plans]
    return [lax.rem(peer - anchors[0] + count, count) for peer in peers]


def put_tile(out, image, place):
    tile_rows = out.shape[0]
    inside = (place >= 0) & (place < APT)

    def put():
        out[...] = image[pl.ds(place * tile_rows, tile_rows)]

    def clear():
        out[...] = jnp.zeros(out.shape, F32)

    pl.when(inside)(put)
    pl.when(jnp.logical_not(inside))(clear)


def inner_kernel(p1, along_y, along_xz, across, lap_p):
    put_laplacian(lap_p, p1[...], along_y, along_xz, across)


def image_kernel(
    plans, anchors, cells, amounts, q0, q1, courant, mixed, lap_p, pair, other, full_p, *refs
):
    outs, image = refs[:-1], refs[-1]
    rows, depth, width = q1.shape
    full_p[...] = lap_p[...]

    def add(span, layers, part):
        full_p[span, layers] = full_p[span, layers] + part

    add_side(pair.at[0 : rows // 2], True, depth, add)
    add_side(other, False, depth, add)

    def row(x, _):
        image[x] = courant[x] * (mixed[x] + q1[x] * full_p[x])
        return 0

    lax.fori_loop(0, rows, row, 0, unroll=4)
    x0 = cells[0, 0]
    here = cell_mask(cells, depth, width)
    added = q0[x0] * jnp.where(here, amounts[0, 0], 0.0) + q1[x0] * jnp.where(here, amounts[0, 1], 0.0)
    image[x0] = image[x0] + added
    for out, place in zip(outs, places(plans, anchors)):
        put_tile(out, image, place)


def last_kernel(
    cells, amounts, p0, p1, q1, courant, lap_p, free_q2, along_y, along_xz, across, pair, other,
    forward_out, adjoint_out, p2, q2, lap_q, sems,
):
    rows, depth, width = p1.shape
    copies = []

    def save(field, out):
        copies.append(pltpu.make_async_copy(field, out, sems.at[len(copies)]))
        copies[-1].start()

    save(p1, forward_out.at[0, 0])
    save(q1, adjoint_out.at[0, 0])

    def row_p(x, _):
        p2[x] = 2.0 * p1[x] - p0[x] + courant[x] * lap_p[x]
        return 0

    lax.fori_loop(0, rows, row_p, 0, unroll=4)
    x0 = cells[0, 0]
    amount = jnp.where(cell_mask(cells, depth, width), amounts[0, 1], 0.0)
    p2[x0] = p2[x0] + amount
    save(p2, forward_out.at[0, 1])
    put_laplacian(lap_q, q1[...], along_y, along_xz, across)

    def add(span, layers, part):
        lap_q[span, layers] = lap_q[span, layers] + part

    add_side(pair.at[rows // 2 :], True, depth, add)
    add_side(other, False, depth, add)

    def row_q(x, _):
        q2[x] = 2.0 * q1[x] + free_q2[x] + courant[x] * lap_q[x]
        return 0

    lax.fori_loop(0, rows, row_q, 0, unroll=4)
    save(q2, adjoint_out.at[0, 1])
    for copy in copies:
        copy.wait()


def gradient_kernel(velocity, *refs):
    parts, out = refs[:-1], refs[-1]
    total = parts[0][...]
    for part in parts[1:]:
        total = total + part[...]
    out[...] = -(2.0 / velocity[...]) * total


def swap(message, start):
    ahead = [(i, i + 1) for i in range(start, lax.axis_size("sub") - 1, 2)]
    return lax.ppermute(message, "sub", ahead + [(i, j) for j, i in ahead])


def on_device(
    velocity, anchors, source_cells, receiver_cells, wavelet, residuals, forward_pair, adjoint_pair
):
    tile_rows, depth, width = velocity.shape
    rows = APT * tile_rows
    receiver_cells = jnp.transpose(receiver_cells, (1, 0, 2))
    field = (rows, depth, width)
    rims = (rows, 2 * RIM, width)
    plans = partners(lax.axis_size("shot"))
    plans_in = [plans[0], *plans[:0:-1]]

    arriving = [lax.ppermute(velocity, "shot", fetch) for fetch, _, _ in plans_in]

    pair, other, p0, q0, tile, cells, amounts = call(
        rims_kernel,
        [given(rims)] * 2 + [kept(field)] * 2 + [kept(velocity.shape)]
        + [pltpu.SMEM(a.shape, a.dtype) for a in (source_cells, wavelet)],
        [(IN_PLACE, in_hbm(a)) for a in (forward_pair, adjoint_pair, velocity, source_cells, wavelet)],
        out_specs=[IN_VMEM] * 5 + [IN_SMEM] * 2,
        scratch=[pltpu.SemaphoreType.DMA((2, 2)), pltpu.SemaphoreType.DMA((3,))],
        name="rims",
    )
    other, pair = swap(other, 1), swap(pair, 0)

    size = min(rows, 256 // depth) * depth
    operators = [
        pltpu.VMEM((2 * width, width), BF16),
        pltpu.VMEM((size, 2 * size), BF16),
        pltpu.VMEM((2, size, 2 * RIM * depth), BF16),
    ]
    free_p, lap_p, free_q, lap_q, free_q2, mixed, *operators = call(
        first_kernel,
        [kept(field)] * 6 + operators,
        [
            (IN_PLACE, in_hbm(receiver_cells)), (IN_PLACE, in_hbm(residuals)),
            (IN_PLACE, in_hbm(forward_pair)), (IN_PLACE, in_hbm(adjoint_pair)),
            (IN_VMEM, on_chip(p0)), (IN_VMEM, on_chip(q0)),
        ],
        scratch=[
            pltpu.VMEM((2,) + field, F32),
            pltpu.VMEM((2,) + field, F32),
            pltpu.VMEM(receiver_cells.shape, jnp.int32),
            pltpu.VMEM(residuals.shape, F32),
            pltpu.SemaphoreType.DMA((2, 2)),
            pltpu.SemaphoreType.DMA((2,)),
        ],
        name="first",
        cost=LONG,
    )
    scalars = [(IN_SMEM, on_smem(cells)), (IN_SMEM, on_smem(amounts))]

    full_p, full_q, mixed = call(
        full_kernel,
        [kept(field)] * 3,
        [(IN_VMEM, on_chip(a)) for a in (lap_p, lap_q, mixed, q0)] + [(IN_VMEM, other), (IN_VMEM, pair)],
        name="full",
    )
    courant, p1, q1, pair, other_p, other_q = call(
        functools.partial(step_kernel, plans_in),
        [kept(field)] * 3 + [given(rims)] + [given((rows // 2, 2 * RIM, width))] * 2,
        [(IN_SMEM, anchors)] + scalars
        + [(IN_VMEM, on_chip(a)) for a in (free_p, free_q, full_p, full_q)]
        + [(IN_VMEM, on_chip(tile))]
        + [(IN_VMEM, other_tile) for other_tile in arriving],
        name="step",
    )
    pair, other_p, other_q = swap(pair, 0), swap(other_p, 1), swap(other_q, 1)

    (lap_p1,) = call(
        inner_kernel,
        [kept(field)],
        [(IN_VMEM, on_chip(a)) for a in (p1, *operators)],
        name="inner",
    )
    lap_p1, *images = call(
        functools.partial(image_kernel, plans),
        [kept(field)] + [given(velocity.shape)] * (len(plans) + 1),
        [(IN_SMEM, anchors)] + scalars
        + [(IN_VMEM, on_chip(a)) for a in (q0, q1, courant, mixed, lap_p1)]
        + [(IN_VMEM, pair), (IN_VMEM, other_p)],
        scratch=[pltpu.VMEM(field, F32)],
        name="image",
    )
    gathered = [images[0]] + [
        lax.ppermute(image, "shot", send) for image, (_, send, _) in zip(images[1:], plans)
    ]

    forward_out, adjoint_out = call(
        last_kernel,
        [given(forward_pair.shape), given(adjoint_pair.shape)],
        scalars
        + [(IN_VMEM, on_chip(a)) for a in (p0, p1, q1, courant, lap_p1, free_q2, *operators)]
        + [(IN_VMEM, pair), (IN_VMEM, other_q)],
        out_specs=[IN_PLACE, IN_PLACE],
        scratch=[pltpu.VMEM(field, F32)] * 3 + [pltpu.SemaphoreType.DMA((4,))],
        name="last",
        cost=LONG,
    )

    (gradient,) = call(
        gradient_kernel,
        [given(velocity.shape)],
        [(IN_VMEM, a) for a in (on_chip(tile), *gathered)],
        name="gradient",
    )
    return gradient, forward_out, adjoint_out


def solution(mesh):
    shot = ("grp", "shot")
    fields = P(shot, None, None, "sub", None)
    return jax.shard_map(
        on_device,
        mesh=mesh,
        in_specs=(
            P(shot, "sub", None),
            P(shot),
            P(shot, None),
            P(shot, None, None),
            P(shot, None),
            P(shot, None, None),
            fields,
            fields,
        ),
        out_specs=(P(shot, "sub", None), fields, fields),
        check_vma=False,
    )
```

```python
import functools

import jax
import jax.numpy as jnp
from jax import lax
from jax.experimental import pallas as pl
from jax.experimental.pallas import tpu as pltpu
from jax.sharding import PartitionSpec as P

APT = 4
RIM = 4
SPACING_RATIO = 0.1
SCALE = 5040
CENTRE = (-43008.0, -42.0)
COEFS = (0.0, 8064.0, -1008.0, 128.0, -9.0)

F32 = jnp.float32
BF16 = jnp.bfloat16
IN_VMEM = pl.BlockSpec(memory_space=pltpu.VMEM)
IN_SMEM = pl.BlockSpec(memory_space=pltpu.SMEM)
IN_PLACE = pl.BlockSpec(memory_space=pltpu.HBM)
LONG = pl.CostEstimate(flops=10**10, bytes_accessed=10**8, transcendentals=0)


def kept(shape):
    return pltpu.VMEM(shape, F32)


def given(shape):
    return jax.ShapeDtypeStruct(shape, F32)


def on_chip(value):
    return pltpu.with_memory_space_constraint(value, pltpu.VMEM)


def on_smem(value):
    return pltpu.with_memory_space_constraint(value, pltpu.SMEM)


def in_hbm(value):
    return pltpu.with_memory_space_constraint(value, pltpu.HBM)


def call(kernel, outs, ins, out_specs=None, scratch=(), name=None, cost=None, aliases=None):
    return pl.pallas_call(
        kernel,
        out_shape=tuple(outs),
        in_specs=[spec for spec, _ in ins],
        out_specs=tuple(out_specs or [IN_VMEM] * len(outs)),
        scratch_shapes=list(scratch),
        compiler_params=pltpu.CompilerParams(vmem_limit_bytes=40 * 1024 * 1024),
        cost_estimate=cost,
        input_output_aliases=aliases or {},
        name=name,
    )(*[array for _, array in ins])


def partners(count):
    reach = APT - 1
    if count <= 2 * reach and count & (count - 1) == 0:
        plans = []
        middle = count // 2
        for bit in [*range(middle, count), *range(1, middle)]:
            pairs = [(i, i ^ bit) for i in range(count)]
            plans.append((pairs, pairs, functools.partial(lambda bit, i: i ^ bit, bit)))
        return plans
    if count <= 2 * reach:
        offsets = range(1, count)
    else:
        offsets = [o for o in range(-reach, reach + 1) if o != 0]
    plans = []
    for o in offsets:
        fetch = [((i + o) % count, i) for i in range(count)]
        send = [(i, (i + o) % count) for i in range(count)]
        plans.append((fetch, send, functools.partial(lambda o, i: lax.rem(i + o + count, count), o)))
    return plans


def coefs_at(apart):
    total = jnp.zeros(apart.shape, F32)
    for o in range(1, RIM + 1):
        total = jnp.where(apart == o, F32(COEFS[o]), total)
    return total


def put_operators(along_y, along_xz, across, depth):
    width, size = along_y.shape[1], along_xz.shape[0]

    def grid(columns):
        row = lax.broadcasted_iota(jnp.int32, (size, columns), 0)
        column = lax.broadcasted_iota(jnp.int32, (size, columns), 1)
        return lax.div(row, depth), lax.rem(row, depth), lax.div(column, depth), lax.rem(column, depth)

    row = lax.broadcasted_iota(jnp.int32, (width, width), 0)
    column = lax.broadcasted_iota(jnp.int32, (width, width), 1)
    value = jnp.where(row == column, F32(CENTRE[1]), coefs_at(jnp.abs(row - column))).astype(BF16)
    along_y[0:width] = value
    along_y[width:] = value

    x, z, other_x, other_z = grid(size)
    same_x, same_z = x == other_x, z == other_z
    value = jnp.where(same_z, coefs_at(jnp.abs(x - other_x)), 0.0)
    value = value + jnp.where(same_x, coefs_at(jnp.abs(z - other_z)), 0.0)
    value = jnp.where(same_x & same_z, F32(CENTRE[0]), value).astype(BF16)
    along_xz[:, 0:size] = value
    along_xz[:, size:] = value

    rim = RIM * depth
    x, z, other_x, other_z = grid(rim)
    for index, first in enumerate((size // depth, -RIM)):
        value = jnp.where(z == other_z, coefs_at(jnp.abs(other_x + first - x)), 0.0).astype(BF16)
        across[index, :, 0:rim] = value
        across[index, :, rim:] = value


def put_laplacian(out, field, along_y, along_xz, across):
    rows, depth, width = field.shape
    flat = field.reshape(rows * depth, width)
    top = flat.astype(BF16)
    rest = (flat - top.astype(F32)).astype(BF16)
    size, rim = along_xz.shape[0], RIM * depth
    for start in range(0, rows * depth, size):
        here = slice(start, start + size)
        left = [top[here], rest[here], along_xz[...]]
        right = [along_y[...], top[here], rest[here]]
        sides = ((0, start + size), (1, start - rim))
        for index, low in sides:
            if 0 <= low < rows * depth:
                left.append(across[index])
                right += [top[low : low + rim], rest[low : low + rim]]
        total = jnp.dot(
            jnp.concatenate(left, axis=1), jnp.concatenate(right, axis=0), preferred_element_type=F32
        )
        out[start // depth : (start + size) // depth] = total.reshape(size // depth, depth, width)


def first_four(shape):
    return lax.broadcasted_iota(jnp.int32, shape, len(shape) - 2) < RIM


def is_even():
    return lax.rem(lax.axis_index("sub"), 2) == 0


def pack_rims(field):
    rows, depth, _ = field.shape
    half = rows // 2
    first, last = field[:, 0 : 2 * RIM], field[:, depth - 2 * RIM : depth]
    here = first_four(first[:half].shape)
    deeper = jnp.where(here, pltpu.roll(last[:half], RIM, 1), last[half:])
    shallower = jnp.where(here, first[:half], pltpu.roll(first[half:], RIM, 1))
    even = is_even()
    return jnp.where(even, deeper, shallower), jnp.where(even, shallower, deeper)


def side_part(message, below, index):
    axis, size = message.ndim - 2, 2 * RIM
    line = lax.broadcasted_iota(jnp.int32, message.shape, axis)
    turn = RIM * (index if below else 1 - index)
    total = None
    for o in range(1, RIM + 1):
        reached = line >= size - o if below else line < o
        shift = (turn + (size - o if below else o)) % size
        moved = pltpu.roll(message, shift, axis) if shift else message
        term = jnp.where(reached, F32(COEFS[o]), 0.0) * moved
        total = term if total is None else total + term
    return total


def add_side(message, pair, depth, add):
    half = message.shape[0]
    for even in (True, False):
        below = pair == even

        def put(below=below):
            layers = slice(depth - 2 * RIM, depth) if below else slice(0, 2 * RIM)
            for index in range(2):
                add(slice(index * half, (index + 1) * half), layers, side_part(message[...], below, index))

        pl.when(is_even() == even)(put)


def cell_mask(cells, depth, width):
    start = lax.axis_index("sub") * depth
    layer = lax.broadcasted_iota(jnp.int32, (depth, width), 0)
    column = lax.broadcasted_iota(jnp.int32, (depth, width), 1)
    return (layer == cells[0, 1] - start) & (column == cells[0, 2])


def load(sources, fields, sems):
    pieces = sems.shape[1]
    copies = []
    for index, (source, field) in enumerate(zip(sources, fields)):
        step = field.shape[0] // pieces
        for piece in range(pieces):
            span = pl.ds(piece * step, step)
            copies.append(pltpu.make_async_copy(source.at[span], field.at[span], sems.at[index, piece]))
    for copy in copies:
        copy.start()
    return copies


def rims_kernel(
    forward, adjoint, velocity, source, wavelet, pair, other, p, q, *refs
):
    onto, (sems, small_sems) = refs[:-2], refs[-2:]
    half = pair.shape[0] // 2
    copies = load((forward.at[0, 1], adjoint.at[0, 1]), (p, q), sems)
    small = [
        pltpu.make_async_copy(source, target, small_sems.at[index])
        for index, (source, target) in enumerate(zip((velocity, source, wavelet), onto))
    ]
    for copy in small:
        copy.start()
    for index, field in enumerate((p, q)):
        for copy in copies[index * len(copies) // 2 : (index + 1) * len(copies) // 2]:
            copy.wait()
        span = slice(index * half, (index + 1) * half)
        pair[span], other[span] = pack_rims(field[...])
    for copy in small:
        copy.wait()


def first_kernel(
    receivers_in, residuals_in, forward, adjoint, p, q,
    free_p, lap_p, free_q, lap_q, free_q2, mixed, along_y, along_xz, across,
    spread, later, receivers, residuals, sems, small_sems,
):
    rows, depth, width = lap_p.shape
    copies = load((forward.at[0, 0], adjoint.at[0, 0]), (later.at[0], later.at[1]), sems)
    small = [
        pltpu.make_async_copy(given_ref, target, small_sems.at[index])
        for index, (given_ref, target) in enumerate(
            ((receivers_in, receivers), (residuals_in, residuals))
        )
    ]
    for copy in small:
        copy.start()
    put_operators(along_y, along_xz, across, depth)
    put_laplacian(lap_p, p[...], along_y, along_xz, across)
    put_laplacian(lap_q, q[...], along_y, along_xz, across)
    for copy in small:
        copy.wait()
    start = lax.axis_index("sub") * depth

    first, layer, column = receivers[0], receivers[1] - start, receivers[2]
    inside = (layer >= 0) & (layer < depth)
    place = jnp.where(inside, first * depth + layer, -1)
    count = place.shape[1]
    lines = lax.broadcasted_iota(jnp.int32, (rows * depth, count), 0)
    onto = (lines == place).astype(F32).astype(BF16)
    columns = lax.broadcasted_iota(jnp.int32, (width, count), 0)
    for step in range(2):
        value = jnp.where(columns == column, residuals[0, step : step + 1], 0.0)
        total = None
        for _ in range(3):
            part = value.astype(BF16)
            value = value - part.astype(F32)
            term = lax.dot_general(onto, part, (((1,), (1,)), ((), ())), preferred_element_type=F32)
            total = term if total is None else total + term
        spread[step] = total.reshape(rows, depth, width)

    for copy in copies:
        copy.wait()

    def row(x, _):
        own = q[x]
        free_p[x] = 2.0 * p[x] - later[0, x]
        free_q[x] = 2.0 * own - later[1, x] + spread[0, x]
        free_q2[x] = spread[1, x] - own
        mixed[x] = own * lap_p[x]
        return 0

    lax.fori_loop(0, rows, row, 0, unroll=4)


def full_kernel(lap_p, lap_q, mixed, now_q, pair, other, full_p, full_q, full_mixed):
    depth = lap_p.shape[1]
    half = pair.shape[0] // 2

    def add_p(span, layers, part):
        full_p[span, layers] = full_p[span, layers] + part
        full_mixed[span, layers] = full_mixed[span, layers] + now_q[span, layers] * part

    def add_q(span, layers, part):
        full_q[span, layers] = full_q[span, layers] + part

    for message, is_pair in ((pair, True), (other, False)):
        add_side(message.at[0:half], is_pair, depth, add_p)
        add_side(message.at[half:], is_pair, depth, add_q)


def step_kernel(plans, anchors, cells, amounts, free_p, free_q, full_p, full_q, *refs):
    tiles, (courant, p1, q1, pair, other_p, other_q) = refs[: len(plans) + 1], refs[len(plans) + 1 :]
    tile_rows = tiles[0].shape[0]
    for tile, place in zip(tiles, places(plans, anchors)):

        def put():
            speed = F32(SPACING_RATIO) * tile[...]
            factor = speed * speed * F32(1.0 / SCALE)
            span = pl.ds(place * tile_rows, tile_rows)
            courant[span] = factor
            p1[span] = free_p[span] + factor * full_p[span]
            q1[span] = free_q[span] + factor * full_q[span]

        pl.when((place >= 0) & (place < APT))(put)
    rows, depth, width = p1.shape
    half = rows // 2
    x0 = cells[0, 0]
    p1[x0] = p1[x0] + jnp.where(cell_mask(cells, depth, width), amounts[0, 0], 0.0)
    pair[0:half], other_p[...] = pack_rims(p1[...])
    pair[half:], other_q[...] = pack_rims(q1[...])


def places(plans, anchors):
    count = lax.axis_size("shot")
    me = lax.axis_index("shot")
    peers = [me] + [peer(me) for _, _, peer in plans]
    return [lax.rem(peer - anchors[0] + count, count) for peer in peers]


def put_tile(out, image, place):
    tile_rows = out.shape[0]
    inside = (place >= 0) & (place < APT)

    def put():
        out[...] = image[pl.ds(place * tile_rows, tile_rows)]

    def clear():
        out[...] = jnp.zeros(out.shape, F32)

    pl.when(inside)(put)
    pl.when(jnp.logical_not(inside))(clear)


def inner_kernel(p1, along_y, along_xz, across, lap_p):
    put_laplacian(lap_p, p1[...], along_y, along_xz, across)


def image_kernel(
    plans, anchors, cells, amounts, q0, q1, courant, mixed, _, pair, other, full_p, *refs
):
    outs, image = refs[:-1], refs[-1]
    rows, depth, width = q1.shape

    def add(span, layers, part):
        full_p[span, layers] = full_p[span, layers] + part

    add_side(pair.at[0 : rows // 2], True, depth, add)
    add_side(other, False, depth, add)

    def row(x, _):
        image[x] = courant[x] * (mixed[x] + q1[x] * full_p[x])
        return 0

    lax.fori_loop(0, rows, row, 0, unroll=4)
    x0 = cells[0, 0]
    here = cell_mask(cells, depth, width)
    added = q0[x0] * jnp.where(here, amounts[0, 0], 0.0) + q1[x0] * jnp.where(here, amounts[0, 1], 0.0)
    image[x0] = image[x0] + added
    for out, place in zip(outs, places(plans, anchors)):
        put_tile(out, image, place)


def last_kernel(
    cells, amounts, p0, p1, q1, courant, lap_p, free_q2, along_y, along_xz, across, pair, other,
    forward_out, adjoint_out, p2, q2, lap_q, sems,
):
    rows, depth, width = p1.shape
    copies = []

    def save(field, out):
        copies.append(pltpu.make_async_copy(field, out, sems.at[len(copies)]))
        copies[-1].start()

    save(p1, forward_out.at[0, 0])
    save(q1, adjoint_out.at[0, 0])

    def row_p(x, _):
        p2[x] = 2.0 * p1[x] - p0[x] + courant[x] * lap_p[x]
        return 0

    lax.fori_loop(0, rows, row_p, 0, unroll=4)
    x0 = cells[0, 0]
    amount = jnp.where(cell_mask(cells, depth, width), amounts[0, 1], 0.0)
    p2[x0] = p2[x0] + amount
    save(p2, forward_out.at[0, 1])
    put_laplacian(lap_q, q1[...], along_y, along_xz, across)

    def add(span, layers, part):
        lap_q[span, layers] = lap_q[span, layers] + part

    add_side(pair.at[rows // 2 :], True, depth, add)
    add_side(other, False, depth, add)

    def row_q(x, _):
        q2[x] = 2.0 * q1[x] + free_q2[x] + courant[x] * lap_q[x]
        return 0

    lax.fori_loop(0, rows, row_q, 0, unroll=4)
    save(q2, adjoint_out.at[0, 1])
    for copy in copies:
        copy.wait()


def gradient_kernel(velocity, *refs):
    parts, out = refs[:-1], refs[-1]
    total = parts[0][...]
    for part in parts[1:]:
        total = total + part[...]
    out[...] = -(2.0 / velocity[...]) * total


def swap(message, start):
    ahead = [(i, i + 1) for i in range(start, lax.axis_size("sub") - 1, 2)]
    return lax.ppermute(message, "sub", ahead + [(i, j) for j, i in ahead])


def on_device(
    velocity, anchors, source_cells, receiver_cells, wavelet, residuals, forward_pair, adjoint_pair
):
    tile_rows, depth, width = velocity.shape
    rows = APT * tile_rows
    receiver_cells = jnp.transpose(receiver_cells, (1, 0, 2))
    field = (rows, depth, width)
    rims = (rows, 2 * RIM, width)
    plans = partners(lax.axis_size("shot"))
    plans_in = [plans[1], plans[2], *plans[3:], plans[0]] if len(plans) == 3 else plans

    arriving = [lax.ppermute(velocity, "shot", fetch) for fetch, _, _ in plans_in]

    pair, other, p0, q0, tile, cells, amounts = call(
        rims_kernel,
        [given(rims)] * 2 + [kept(field)] * 2 + [kept(velocity.shape)]
        + [pltpu.SMEM(a.shape, a.dtype) for a in (source_cells, wavelet)],
        [(IN_PLACE, in_hbm(a)) for a in (forward_pair, adjoint_pair, velocity, source_cells, wavelet)],
        out_specs=[IN_VMEM] * 5 + [IN_SMEM] * 2,
        scratch=[pltpu.SemaphoreType.DMA((2, 2)), pltpu.SemaphoreType.DMA((3,))],
        name="rims",
    )
    pair, other = swap(pair, 0), swap(other, 1)

    size = min(rows, 256 // depth) * depth
    operators = [
        pltpu.VMEM((2 * width, width), BF16),
        pltpu.VMEM((size, 2 * size), BF16),
        pltpu.VMEM((2, size, 2 * RIM * depth), BF16),
    ]
    free_p, lap_p, free_q, lap_q, free_q2, mixed, *operators = call(
        first_kernel,
        [kept(field)] * 6 + operators,
        [
            (IN_PLACE, in_hbm(receiver_cells)), (IN_PLACE, in_hbm(residuals)),
            (IN_PLACE, in_hbm(forward_pair)), (IN_PLACE, in_hbm(adjoint_pair)),
            (IN_VMEM, on_chip(p0)), (IN_VMEM, on_chip(q0)),
        ],
        scratch=[
            pltpu.VMEM((2,) + field, F32),
            pltpu.VMEM((2,) + field, F32),
            pltpu.VMEM(receiver_cells.shape, jnp.int32),
            pltpu.VMEM(residuals.shape, F32),
            pltpu.SemaphoreType.DMA((2, 2)),
            pltpu.SemaphoreType.DMA((2,)),
        ],
        name="first",
        cost=LONG,
    )
    scalars = [(IN_SMEM, on_smem(cells)), (IN_SMEM, on_smem(amounts))]

    full_p, full_q, mixed = call(
        full_kernel,
        [kept(field)] * 3,
        [(IN_VMEM, on_chip(a)) for a in (lap_p, lap_q, mixed, q0)] + [(IN_VMEM, pair), (IN_VMEM, other)],
        name="full",
        aliases={0: 0, 1: 1, 2: 2},
    )
    courant, p1, q1, pair, other_p, other_q = call(
        functools.partial(step_kernel, plans_in),
        [kept(field)] * 3 + [given(rims)] + [given((rows // 2, 2 * RIM, width))] * 2,
        [(IN_SMEM, anchors)] + scalars
        + [(IN_VMEM, on_chip(a)) for a in (free_p, free_q, full_p, full_q)]
        + [(IN_VMEM, on_chip(tile))]
        + [(IN_VMEM, other_tile) for other_tile in arriving],
        name="step",
    )
    pair, other_p, other_q = swap(pair, 0), swap(other_p, 1), swap(other_q, 1)

    (lap_p1,) = call(
        inner_kernel,
        [kept(field)],
        [(IN_VMEM, on_chip(a)) for a in (p1, *operators)],
        name="inner",
    )
    lap_p1, *images = call(
        functools.partial(image_kernel, plans),
        [kept(field)] + [given(velocity.shape)] * (len(plans) + 1),
        [(IN_SMEM, anchors)] + scalars
        + [(IN_VMEM, on_chip(a)) for a in (q0, q1, courant, mixed, lap_p1)]
        + [(IN_VMEM, pair), (IN_VMEM, other_p)],
        scratch=[pltpu.VMEM(field, F32)],
        name="image",
        aliases={7: 0},
    )
    gathered = [images[0]] + [
        lax.ppermute(image, "shot", send) for image, (_, send, _) in zip(images[1:], plans)
    ]

    forward_out, adjoint_out = call(
        last_kernel,
        [given(forward_pair.shape), given(adjoint_pair.shape)],
        scalars
        + [(IN_VMEM, on_chip(a)) for a in (p0, p1, q1, courant, lap_p1, free_q2, *operators)]
        + [(IN_VMEM, pair), (IN_VMEM, other_q)],
        out_specs=[IN_PLACE, IN_PLACE],
        scratch=[pltpu.VMEM(field, F32)] * 3 + [pltpu.SemaphoreType.DMA((4,))],
        name="last",
        cost=LONG,
    )

    (gradient,) = call(
        gradient_kernel,
        [given(velocity.shape)],
        [(IN_VMEM, a) for a in (on_chip(tile), *gathered)],
        name="gradient",
    )
    return gradient, forward_out, adjoint_out


def solution(mesh):
    shot = ("grp", "shot")
    fields = P(shot, None, None, "sub", None)
    return jax.shard_map(
        on_device,
        mesh=mesh,
        in_specs=(
            P(shot, "sub", None),
            P(shot),
            P(shot, None),
            P(shot, None, None),
            P(shot, None),
            P(shot, None, None),
            fields,
            fields,
        ),
        out_specs=(P(shot, "sub", None), fields, fields),
        check_vma=False,
    )
```

```python
import functools

import jax
import jax.numpy as jnp
from jax import lax
from jax.experimental import pallas as pl
from jax.experimental.pallas import tpu as pltpu
from jax.sharding import PartitionSpec as P

APT = 4
RIM = 4
SPACING_RATIO = 0.1
SCALE = 5040
CENTRE = (-43008.0, -42.0)
COEFS = (0.0, 8064.0, -1008.0, 128.0, -9.0)

F32 = jnp.float32
BF16 = jnp.bfloat16
IN_VMEM = pl.BlockSpec(memory_space=pltpu.VMEM)
IN_SMEM = pl.BlockSpec(memory_space=pltpu.SMEM)
IN_PLACE = pl.BlockSpec(memory_space=pltpu.HBM)
LONG = pl.CostEstimate(flops=10**10, bytes_accessed=10**8, transcendentals=0)


def kept(shape):
    return pltpu.VMEM(shape, F32)


def given(shape):
    return jax.ShapeDtypeStruct(shape, F32)


def on_chip(value):
    return pltpu.with_memory_space_constraint(value, pltpu.VMEM)


def on_smem(value):
    return pltpu.with_memory_space_constraint(value, pltpu.SMEM)


def in_hbm(value):
    return pltpu.with_memory_space_constraint(value, pltpu.HBM)


def call(kernel, outs, ins, out_specs=None, scratch=(), name=None, cost=None, aliases=None):
    return pl.pallas_call(
        kernel,
        out_shape=tuple(outs),
        in_specs=[spec for spec, _ in ins],
        out_specs=tuple(out_specs or [IN_VMEM] * len(outs)),
        scratch_shapes=list(scratch),
        compiler_params=pltpu.CompilerParams(vmem_limit_bytes=40 * 1024 * 1024),
        cost_estimate=cost,
        input_output_aliases=aliases or {},
        name=name,
    )(*[array for _, array in ins])


def partners(count):
    reach = APT - 1
    if count <= 2 * reach and count & (count - 1) == 0:
        plans = []
        middle = count // 2
        for bit in [*range(middle, count), *range(1, middle)]:
            pairs = [(i, i ^ bit) for i in range(count)]
            plans.append((pairs, pairs, functools.partial(lambda bit, i: i ^ bit, bit)))
        return plans
    if count <= 2 * reach:
        offsets = range(1, count)
    else:
        offsets = [o for o in range(-reach, reach + 1) if o != 0]
    plans = []
    for o in offsets:
        fetch = [((i + o) % count, i) for i in range(count)]
        send = [(i, (i + o) % count) for i in range(count)]
        plans.append((fetch, send, functools.partial(lambda o, i: lax.rem(i + o + count, count), o)))
    return plans


def coefs_at(apart):
    total = jnp.zeros(apart.shape, F32)
    for o in range(1, RIM + 1):
        total = jnp.where(apart == o, F32(COEFS[o]), total)
    return total


def put_operators(along_y, along_xz, across, depth):
    width, size = along_y.shape[1], along_xz.shape[0]

    def grid(columns):
        row = lax.broadcasted_iota(jnp.int32, (size, columns), 0)
        column = lax.broadcasted_iota(jnp.int32, (size, columns), 1)
        return lax.div(row, depth), lax.rem(row, depth), lax.div(column, depth), lax.rem(column, depth)

    row = lax.broadcasted_iota(jnp.int32, (width, width), 0)
    column = lax.broadcasted_iota(jnp.int32, (width, width), 1)
    value = jnp.where(row == column, F32(CENTRE[1]), coefs_at(jnp.abs(row - column))).astype(BF16)
    along_y[0:width] = value
    along_y[width:] = value

    x, z, other_x, other_z = grid(size)
    same_x, same_z = x == other_x, z == other_z
    value = jnp.where(same_z, coefs_at(jnp.abs(x - other_x)), 0.0)
    value = value + jnp.where(same_x, coefs_at(jnp.abs(z - other_z)), 0.0)
    value = jnp.where(same_x & same_z, F32(CENTRE[0]), value).astype(BF16)
    along_xz[:, 0:size] = value
    along_xz[:, size:] = value

    rim = RIM * depth
    x, z, other_x, other_z = grid(rim)
    for index, first in enumerate((size // depth, -RIM)):
        value = jnp.where(z == other_z, coefs_at(jnp.abs(other_x + first - x)), 0.0).astype(BF16)
        across[index, :, 0:rim] = value
        across[index, :, rim:] = value


def put_laplacian(out, field, along_y, along_xz, across):
    rows, depth, width = field.shape
    flat = field.reshape(rows * depth, width)
    top = flat.astype(BF16)
    rest = (flat - top.astype(F32)).astype(BF16)
    size, rim = along_xz.shape[0], RIM * depth
    for start in range(0, rows * depth, size):
        here = slice(start, start + size)
        left = [top[here], rest[here], along_xz[...]]
        right = [along_y[...], top[here], rest[here]]
        sides = ((0, start + size), (1, start - rim))
        for index, low in sides:
            if 0 <= low < rows * depth:
                left.append(across[index])
                right += [top[low : low + rim], rest[low : low + rim]]
        total = jnp.dot(
            jnp.concatenate(left, axis=1), jnp.concatenate(right, axis=0), preferred_element_type=F32
        )
        out[start // depth : (start + size) // depth] = total.reshape(size // depth, depth, width)


def first_four(shape):
    return lax.broadcasted_iota(jnp.int32, shape, len(shape) - 2) < RIM


def is_even():
    return lax.rem(lax.axis_index("sub"), 2) == 0


def pack_rims(field):
    rows, depth, _ = field.shape
    half = rows // 2
    first, last = field[:, 0 : 2 * RIM], field[:, depth - 2 * RIM : depth]
    here = first_four(first[:half].shape)
    deeper = jnp.where(here, pltpu.roll(last[:half], RIM, 1), last[half:])
    shallower = jnp.where(here, first[:half], pltpu.roll(first[half:], RIM, 1))
    even = is_even()
    return jnp.where(even, deeper, shallower), jnp.where(even, shallower, deeper)


def side_part(message, below, index):
    axis, size = message.ndim - 2, 2 * RIM
    line = lax.broadcasted_iota(jnp.int32, message.shape, axis)
    turn = RIM * (index if below else 1 - index)
    total = None
    for o in range(1, RIM + 1):
        reached = line >= size - o if below else line < o
        shift = (turn + (size - o if below else o)) % size
        moved = pltpu.roll(message, shift, axis) if shift else message
        term = jnp.where(reached, F32(COEFS[o]), 0.0) * moved
        total = term if total is None else total + term
    return total


def add_side(message, pair, depth, add):
    half = message.shape[0]
    for even in (True, False):
        below = pair == even

        def put(below=below):
            layers = slice(depth - 2 * RIM, depth) if below else slice(0, 2 * RIM)
            for index in range(2):
                add(slice(index * half, (index + 1) * half), layers, side_part(message[...], below, index))

        pl.when(is_even() == even)(put)


def cell_mask(cells, depth, width):
    start = lax.axis_index("sub") * depth
    layer = lax.broadcasted_iota(jnp.int32, (depth, width), 0)
    column = lax.broadcasted_iota(jnp.int32, (depth, width), 1)
    return (layer == cells[0, 1] - start) & (column == cells[0, 2])


def load(sources, fields, sems):
    pieces = sems.shape[1]
    copies = []
    for index, (source, field) in enumerate(zip(sources, fields)):
        step = field.shape[0] // pieces
        for piece in range(pieces):
            span = pl.ds(piece * step, step)
            copies.append(pltpu.make_async_copy(source.at[span], field.at[span], sems.at[index, piece]))
    for copy in copies:
        copy.start()
    return copies


def rims_kernel(
    forward, adjoint, velocity, source, wavelet, pair, other, p, q, *refs
):
    onto, (sems, small_sems) = refs[:-2], refs[-2:]
    half = pair.shape[0] // 2
    copies = load((forward.at[0, 1], adjoint.at[0, 1]), (p, q), sems)
    small = [
        pltpu.make_async_copy(source, target, small_sems.at[index])
        for index, (source, target) in enumerate(zip((velocity, source, wavelet), onto))
    ]
    for copy in small:
        copy.start()
    for index, field in enumerate((p, q)):
        for copy in copies[index * len(copies) // 2 : (index + 1) * len(copies) // 2]:
            copy.wait()
        span = slice(index * half, (index + 1) * half)
        pair[span], other[span] = pack_rims(field[...])
    for copy in small:
        copy.wait()


def first_kernel(
    receivers_in, residuals_in, forward, adjoint, p, q,
    free_p, lap_p, free_q, lap_q, free_q2, mixed, along_y, along_xz, across,
    spread, later, receivers, residuals, sems, small_sems,
):
    rows, depth, width = lap_p.shape
    copies = load((forward.at[0, 0], adjoint.at[0, 0]), (later.at[0], later.at[1]), sems)
    small = [
        pltpu.make_async_copy(given_ref, target, small_sems.at[index])
        for index, (given_ref, target) in enumerate(
            ((receivers_in, receivers), (residuals_in, residuals))
        )
    ]
    for copy in small:
        copy.start()
    put_operators(along_y, along_xz, across, depth)
    put_laplacian(lap_p, p[...], along_y, along_xz, across)
    put_laplacian(lap_q, q[...], along_y, along_xz, across)
    for copy in small:
        copy.wait()
    start = lax.axis_index("sub") * depth

    first, layer, column = receivers[0], receivers[1] - start, receivers[2]
    inside = (layer >= 0) & (layer < depth)
    place = jnp.where(inside, first * depth + layer, -1)
    count = place.shape[1]
    lines = lax.broadcasted_iota(jnp.int32, (rows * depth, count), 0)
    onto = (lines == place).astype(F32).astype(BF16)
    columns = lax.broadcasted_iota(jnp.int32, (width, count), 0)
    for step in range(2):
        value = jnp.where(columns == column, residuals[0, step : step + 1], 0.0)
        total = None
        for _ in range(3):
            part = value.astype(BF16)
            value = value - part.astype(F32)
            term = lax.dot_general(onto, part, (((1,), (1,)), ((), ())), preferred_element_type=F32)
            total = term if total is None else total + term
        spread[step] = total.reshape(rows, depth, width)

    for copy in copies:
        copy.wait()

    def row(x, _):
        own = q[x]
        free_p[x] = 2.0 * p[x] - later[0, x]
        free_q[x] = 2.0 * own - later[1, x] + spread[0, x]
        free_q2[x] = spread[1, x] - own
        mixed[x] = own * lap_p[x]
        return 0

    lax.fori_loop(0, rows, row, 0, unroll=4)


def full_kernel(lap_p, lap_q, mixed, now_q, pair, other, full_p, full_q, full_mixed):
    depth = lap_p.shape[1]
    half = pair.shape[0] // 2

    def add_p(span, layers, part):
        full_p[span, layers] = full_p[span, layers] + part
        full_mixed[span, layers] = full_mixed[span, layers] + now_q[span, layers] * part

    def add_q(span, layers, part):
        full_q[span, layers] = full_q[span, layers] + part

    for message, is_pair in ((pair, True), (other, False)):
        add_side(message.at[0:half], is_pair, depth, add_p)
        add_side(message.at[half:], is_pair, depth, add_q)


def step_kernel(plans, anchors, cells, amounts, free_p, free_q, full_p, full_q, *refs):
    tiles, (courant, p1, q1, pair, other_p, other_q) = refs[: len(plans) + 1], refs[len(plans) + 1 :]
    tile_rows = tiles[0].shape[0]
    for tile, place in zip(tiles, places(plans, anchors)):

        def put():
            speed = F32(SPACING_RATIO) * tile[...]
            factor = speed * speed * F32(1.0 / SCALE)
            span = pl.ds(place * tile_rows, tile_rows)
            courant[span] = factor
            p1[span] = free_p[span] + factor * full_p[span]
            q1[span] = free_q[span] + factor * full_q[span]

        pl.when((place >= 0) & (place < APT))(put)
    rows, depth, width = p1.shape
    half = rows // 2
    x0 = cells[0, 0]
    p1[x0] = p1[x0] + jnp.where(cell_mask(cells, depth, width), amounts[0, 0], 0.0)
    pair[0:half], other_p[...] = pack_rims(p1[...])
    pair[half:], other_q[...] = pack_rims(q1[...])


def places(plans, anchors):
    count = lax.axis_size("shot")
    me = lax.axis_index("shot")
    peers = [me] + [peer(me) for _, _, peer in plans]
    return [lax.rem(peer - anchors[0] + count, count) for peer in peers]


def inner_kernel(p1, along_y, along_xz, across, lap_p):
    put_laplacian(lap_p, p1[...], along_y, along_xz, across)


def image_kernel(
    plans, anchors, cells, amounts, q0, q1, courant, mixed, _, pair, other, full_p, *refs
):
    outs = refs
    rows, depth, width = q1.shape

    def add(span, layers, part):
        full_p[span, layers] = full_p[span, layers] + part

    add_side(pair.at[0 : rows // 2], True, depth, add)
    add_side(other, False, depth, add)

    x0 = cells[0, 0]
    here = cell_mask(cells, depth, width)
    added = q0[x0] * jnp.where(here, amounts[0, 0], 0.0) + q1[x0] * jnp.where(here, amounts[0, 1], 0.0)
    tile_rows = outs[0].shape[0]
    for out, place in zip(outs, places(plans, anchors)):
        inside = (place >= 0) & (place < APT)
        start = place * tile_rows

        def put():
            for row in range(tile_rows):
                x = start + row
                out[row] = courant[x] * (mixed[x] + q1[x] * full_p[x]) + jnp.where(x == x0, added, 0.0)

        def clear():
            out[...] = jnp.zeros(out.shape, F32)

        pl.when(inside)(put)
        pl.when(jnp.logical_not(inside))(clear)


def last_kernel(
    cells, amounts, p0, p1, q1, courant, lap_p, free_q2, along_y, along_xz, across, pair, other,
    forward_out, adjoint_out, p2, q2, lap_q, sems,
):
    rows, depth, width = p1.shape
    copies = []

    def save(field, out):
        copies.append(pltpu.make_async_copy(field, out, sems.at[len(copies)]))
        copies[-1].start()

    save(p1, forward_out.at[0, 0])
    save(q1, adjoint_out.at[0, 0])

    def row_p(x, _):
        p2[x] = 2.0 * p1[x] - p0[x] + courant[x] * lap_p[x]
        return 0

    lax.fori_loop(0, rows, row_p, 0, unroll=4)
    x0 = cells[0, 0]
    amount = jnp.where(cell_mask(cells, depth, width), amounts[0, 1], 0.0)
    p2[x0] = p2[x0] + amount
    save(p2, forward_out.at[0, 1])
    put_laplacian(lap_q, q1[...], along_y, along_xz, across)

    def add(span, layers, part):
        lap_q[span, layers] = lap_q[span, layers] + part

    add_side(pair.at[rows // 2 :], True, depth, add)
    add_side(other, False, depth, add)

    def row_q(x, _):
        q2[x] = 2.0 * q1[x] + free_q2[x] + courant[x] * lap_q[x]
        return 0

    lax.fori_loop(0, rows, row_q, 0, unroll=4)
    save(q2, adjoint_out.at[0, 1])
    for copy in copies:
        copy.wait()


def gradient_kernel(velocity, *refs):
    parts, out = refs[:-1], refs[-1]
    total = parts[0][...]
    for part in parts[1:]:
        total = total + part[...]
    out[...] = -(2.0 / velocity[...]) * total


def swap(message, start):
    ahead = [(i, i + 1) for i in range(start, lax.axis_size("sub") - 1, 2)]
    return lax.ppermute(message, "sub", ahead + [(i, j) for j, i in ahead])


def on_device(
    velocity, anchors, source_cells, receiver_cells, wavelet, residuals, forward_pair, adjoint_pair
):
    tile_rows, depth, width = velocity.shape
    rows = APT * tile_rows
    receiver_cells = jnp.transpose(receiver_cells, (1, 0, 2))
    field = (rows, depth, width)
    rims = (rows, 2 * RIM, width)
    plans = partners(lax.axis_size("shot"))
    plans_in = [plans[1], plans[2], *plans[3:], plans[0]] if len(plans) == 3 else plans

    arriving = [lax.ppermute(velocity, "shot", fetch) for fetch, _, _ in plans_in]

    pair, other, p0, q0, tile, cells, amounts = call(
        rims_kernel,
        [given(rims)] * 2 + [kept(field)] * 2 + [kept(velocity.shape)]
        + [pltpu.SMEM(a.shape, a.dtype) for a in (source_cells, wavelet)],
        [(IN_PLACE, in_hbm(a)) for a in (forward_pair, adjoint_pair, velocity, source_cells, wavelet)],
        out_specs=[IN_VMEM] * 5 + [IN_SMEM] * 2,
        scratch=[pltpu.SemaphoreType.DMA((2, 2)), pltpu.SemaphoreType.DMA((3,))],
        name="rims",
    )
    pair, other = swap(pair, 0), swap(other, 1)

    size = min(rows, 256 // depth) * depth
    operators = [
        pltpu.VMEM((2 * width, width), BF16),
        pltpu.VMEM((size, 2 * size), BF16),
        pltpu.VMEM((2, size, 2 * RIM * depth), BF16),
    ]
    free_p, lap_p, free_q, lap_q, free_q2, mixed, *operators = call(
        first_kernel,
        [kept(field)] * 6 + operators,
        [
            (IN_PLACE, in_hbm(receiver_cells)), (IN_PLACE, in_hbm(residuals)),
            (IN_PLACE, in_hbm(forward_pair)), (IN_PLACE, in_hbm(adjoint_pair)),
            (IN_VMEM, on_chip(p0)), (IN_VMEM, on_chip(q0)),
        ],
        scratch=[
            pltpu.VMEM((2,) + field, F32),
            pltpu.VMEM((2,) + field, F32),
            pltpu.VMEM(receiver_cells.shape, jnp.int32),
            pltpu.VMEM(residuals.shape, F32),
            pltpu.SemaphoreType.DMA((2, 2)),
            pltpu.SemaphoreType.DMA((2,)),
        ],
        name="first",
        cost=LONG,
    )
    scalars = [(IN_SMEM, on_smem(cells)), (IN_SMEM, on_smem(amounts))]

    full_p, full_q, mixed = call(
        full_kernel,
        [kept(field)] * 3,
        [(IN_VMEM, on_chip(a)) for a in (lap_p, lap_q, mixed, q0)] + [(IN_VMEM, pair), (IN_VMEM, other)],
        name="full",
        aliases={0: 0, 1: 1, 2: 2},
    )
    courant, p1, q1, pair, other_p, other_q = call(
        functools.partial(step_kernel, plans_in),
        [kept(field)] * 3 + [given(rims)] + [given((rows // 2, 2 * RIM, width))] * 2,
        [(IN_SMEM, anchors)] + scalars
        + [(IN_VMEM, on_chip(a)) for a in (free_p, free_q, full_p, full_q)]
        + [(IN_VMEM, on_chip(tile))]
        + [(IN_VMEM, other_tile) for other_tile in arriving],
        name="step",
    )
    pair, other_p, other_q = swap(pair, 0), swap(other_p, 1), swap(other_q, 1)

    (lap_p1,) = call(
        inner_kernel,
        [kept(field)],
        [(IN_VMEM, on_chip(a)) for a in (p1, *operators)],
        name="inner",
    )
    lap_p1, *images = call(
        functools.partial(image_kernel, plans),
        [kept(field)] + [given(velocity.shape)] * (len(plans) + 1),
        [(IN_SMEM, anchors)] + scalars
        + [(IN_VMEM, on_chip(a)) for a in (q0, q1, courant, mixed, lap_p1)]
        + [(IN_VMEM, pair), (IN_VMEM, other_p)],
        name="image",
        aliases={7: 0},
    )
    gathered = [images[0]] + [
        lax.ppermute(image, "shot", send) for image, (_, send, _) in zip(images[1:], plans)
    ]

    forward_out, adjoint_out = call(
        last_kernel,
        [given(forward_pair.shape), given(adjoint_pair.shape)],
        scalars
        + [(IN_VMEM, on_chip(a)) for a in (p0, p1, q1, courant, lap_p1, free_q2, *operators)]
        + [(IN_VMEM, pair), (IN_VMEM, other_q)],
        out_specs=[IN_PLACE, IN_PLACE],
        scratch=[pltpu.VMEM(field, F32)] * 3 + [pltpu.SemaphoreType.DMA((4,))],
        name="last",
        cost=LONG,
    )

    (gradient,) = call(
        gradient_kernel,
        [given(velocity.shape)],
        [(IN_VMEM, a) for a in (on_chip(tile), *gathered)],
        name="gradient",
    )
    return gradient, forward_out, adjoint_out


def solution(mesh):
    shot = ("grp", "shot")
    fields = P(shot, None, None, "sub", None)
    return jax.shard_map(
        on_device,
        mesh=mesh,
        in_specs=(
            P(shot, "sub", None),
            P(shot),
            P(shot, None),
            P(shot, None, None),
            P(shot, None),
            P(shot, None, None),
            fields,
            fields,
        ),
        out_specs=(P(shot, "sub", None), fields, fields),
        check_vma=False,
    )
```

```python
import functools

import jax
import jax.numpy as jnp
from jax import lax
from jax.experimental import pallas as pl
from jax.experimental.pallas import tpu as pltpu
from jax.sharding import PartitionSpec as P

APT = 4
RIM = 4
SPACING_RATIO = 0.1
SCALE = 5040
CENTRE = (-43008.0, -42.0)
COEFS = (0.0, 8064.0, -1008.0, 128.0, -9.0)

F32 = jnp.float32
BF16 = jnp.bfloat16
IN_VMEM = pl.BlockSpec(memory_space=pltpu.VMEM)
IN_SMEM = pl.BlockSpec(memory_space=pltpu.SMEM)
IN_PLACE = pl.BlockSpec(memory_space=pltpu.HBM)
LONG = pl.CostEstimate(flops=10**10, bytes_accessed=10**8, transcendentals=0)


def kept(shape):
    return pltpu.VMEM(shape, F32)


def given(shape):
    return jax.ShapeDtypeStruct(shape, F32)


def on_chip(value):
    return pltpu.with_memory_space_constraint(value, pltpu.VMEM)


def on_smem(value):
    return pltpu.with_memory_space_constraint(value, pltpu.SMEM)


def in_hbm(value):
    return pltpu.with_memory_space_constraint(value, pltpu.HBM)


def call(kernel, outs, ins, out_specs=None, scratch=(), name=None, cost=None, aliases=None):
    return pl.pallas_call(
        kernel,
        out_shape=tuple(outs),
        in_specs=[spec for spec, _ in ins],
        out_specs=tuple(out_specs or [IN_VMEM] * len(outs)),
        scratch_shapes=list(scratch),
        compiler_params=pltpu.CompilerParams(vmem_limit_bytes=40 * 1024 * 1024),
        cost_estimate=cost,
        input_output_aliases=aliases or {},
        name=name,
    )(*[array for _, array in ins])


def partners(count):
    reach = APT - 1
    if count <= 2 * reach and count & (count - 1) == 0:
        plans = []
        middle = count // 2
        for bit in [*range(middle, count), *range(1, middle)]:
            pairs = [(i, i ^ bit) for i in range(count)]
            plans.append((pairs, pairs, functools.partial(lambda bit, i: i ^ bit, bit)))
        return plans
    if count <= 2 * reach:
        offsets = range(1, count)
    else:
        offsets = [o for o in range(-reach, reach + 1) if o != 0]
    plans = []
    for o in offsets:
        fetch = [((i + o) % count, i) for i in range(count)]
        send = [(i, (i + o) % count) for i in range(count)]
        plans.append((fetch, send, functools.partial(lambda o, i: lax.rem(i + o + count, count), o)))
    return plans


def coefs_at(apart):
    total = jnp.zeros(apart.shape, F32)
    for o in range(1, RIM + 1):
        total = jnp.where(apart == o, F32(COEFS[o]), total)
    return total


def put_operators(along_y, along_xz, across, depth):
    width, size = along_y.shape[1], along_xz.shape[0]

    def grid(columns):
        row = lax.broadcasted_iota(jnp.int32, (size, columns), 0)
        column = lax.broadcasted_iota(jnp.int32, (size, columns), 1)
        return lax.div(row, depth), lax.rem(row, depth), lax.div(column, depth), lax.rem(column, depth)

    row = lax.broadcasted_iota(jnp.int32, (width, width), 0)
    column = lax.broadcasted_iota(jnp.int32, (width, width), 1)
    value = jnp.where(row == column, F32(CENTRE[1]), coefs_at(jnp.abs(row - column))).astype(BF16)
    along_y[0:width] = value
    along_y[width:] = value

    x, z, other_x, other_z = grid(size)
    same_x, same_z = x == other_x, z == other_z
    value = jnp.where(same_z, coefs_at(jnp.abs(x - other_x)), 0.0)
    value = value + jnp.where(same_x, coefs_at(jnp.abs(z - other_z)), 0.0)
    value = jnp.where(same_x & same_z, F32(CENTRE[0]), value).astype(BF16)
    along_xz[:, 0:size] = value
    along_xz[:, size:] = value

    rim = RIM * depth
    x, z, other_x, other_z = grid(rim)
    for index, first in enumerate((size // depth, -RIM)):
        value = jnp.where(z == other_z, coefs_at(jnp.abs(other_x + first - x)), 0.0).astype(BF16)
        across[index, :, 0:rim] = value
        across[index, :, rim:] = value


def put_laplacian(out, field, along_y, along_xz, across):
    rows, depth, width = field.shape
    flat = field.reshape(rows * depth, width)
    top = flat.astype(BF16)
    rest = (flat - top.astype(F32)).astype(BF16)
    size, rim = along_xz.shape[0], RIM * depth
    for start in range(0, rows * depth, size):
        here = slice(start, start + size)
        left = [top[here], rest[here], along_xz[...]]
        right = [along_y[...], top[here], rest[here]]
        sides = ((0, start + size), (1, start - rim))
        for index, low in sides:
            if 0 <= low < rows * depth:
                left.append(across[index])
                right += [top[low : low + rim], rest[low : low + rim]]
        total = jnp.dot(
            jnp.concatenate(left, axis=1), jnp.concatenate(right, axis=0), preferred_element_type=F32
        )
        out[start // depth : (start + size) // depth] = total.reshape(size // depth, depth, width)


def first_four(shape):
    return lax.broadcasted_iota(jnp.int32, shape, len(shape) - 2) < RIM


def is_even():
    return lax.rem(lax.axis_index("sub"), 2) == 0


def pack_rims(field):
    rows, depth, _ = field.shape
    half = rows // 2
    first, last = field[:, 0 : 2 * RIM], field[:, depth - 2 * RIM : depth]
    here = first_four(first[:half].shape)
    deeper = jnp.where(here, pltpu.roll(last[:half], RIM, 1), last[half:])
    shallower = jnp.where(here, first[:half], pltpu.roll(first[half:], RIM, 1))
    even = is_even()
    return jnp.where(even, deeper, shallower), jnp.where(even, shallower, deeper)


def side_part(message, below, index):
    axis, size = message.ndim - 2, 2 * RIM
    line = lax.broadcasted_iota(jnp.int32, message.shape, axis)
    turn = RIM * (index if below else 1 - index)
    total = None
    for o in range(1, RIM + 1):
        reached = line >= size - o if below else line < o
        shift = (turn + (size - o if below else o)) % size
        moved = pltpu.roll(message, shift, axis) if shift else message
        term = jnp.where(reached, F32(COEFS[o]), 0.0) * moved
        total = term if total is None else total + term
    return total


def add_side(message, pair, depth, add):
    half = message.shape[0]
    for even in (True, False):
        below = pair == even

        def put(below=below):
            layers = slice(depth - 2 * RIM, depth) if below else slice(0, 2 * RIM)
            for index in range(2):
                add(slice(index * half, (index + 1) * half), layers, side_part(message[...], below, index))

        pl.when(is_even() == even)(put)


def cell_mask(cells, depth, width):
    start = lax.axis_index("sub") * depth
    layer = lax.broadcasted_iota(jnp.int32, (depth, width), 0)
    column = lax.broadcasted_iota(jnp.int32, (depth, width), 1)
    return (layer == cells[0, 1] - start) & (column == cells[0, 2])


def load(sources, fields, sems):
    pieces = sems.shape[1]
    copies = []
    for index, (source, field) in enumerate(zip(sources, fields)):
        step = field.shape[0] // pieces
        for piece in range(pieces):
            span = pl.ds(piece * step, step)
            copies.append(pltpu.make_async_copy(source.at[span], field.at[span], sems.at[index, piece]))
    for copy in copies:
        copy.start()
    return copies


def rims_kernel(
    forward, adjoint, velocity, source, wavelet, pair, other, p, q, *refs
):
    onto, (sems, small_sems) = refs[:-2], refs[-2:]
    half = pair.shape[0] // 2
    copies = load((forward.at[0, 1], adjoint.at[0, 1]), (p, q), sems)
    small = [
        pltpu.make_async_copy(source, target, small_sems.at[index])
        for index, (source, target) in enumerate(zip((velocity, source, wavelet), onto))
    ]
    for copy in small:
        copy.start()
    for index, field in enumerate((p, q)):
        for copy in copies[index * len(copies) // 2 : (index + 1) * len(copies) // 2]:
            copy.wait()
        span = slice(index * half, (index + 1) * half)
        pair[span], other[span] = pack_rims(field[...])
    for copy in small:
        copy.wait()


def first_kernel(
    receivers_in, residuals_in, forward, adjoint, p, q,
    free_p, lap_p, free_q, lap_q, free_q2, mixed, along_y, along_xz, across,
    spread, later, receivers, residuals, sems, small_sems,
):
    rows, depth, width = lap_p.shape
    copies = load((forward.at[0, 0], adjoint.at[0, 0]), (later.at[0], later.at[1]), sems)
    small = [
        pltpu.make_async_copy(given_ref, target, small_sems.at[index])
        for index, (given_ref, target) in enumerate(
            ((receivers_in, receivers), (residuals_in, residuals))
        )
    ]
    for copy in small:
        copy.start()
    put_operators(along_y, along_xz, across, depth)
    put_laplacian(lap_p, p[...], along_y, along_xz, across)
    put_laplacian(lap_q, q[...], along_y, along_xz, across)
    for copy in small:
        copy.wait()
    start = lax.axis_index("sub") * depth

    first, layer, column = receivers[0], receivers[1] - start, receivers[2]
    inside = (layer >= 0) & (layer < depth)
    place = jnp.where(inside, first * depth + layer, -1)
    count = place.shape[1]
    lines = lax.broadcasted_iota(jnp.int32, (rows * depth, count), 0)
    onto = (lines == place).astype(F32).astype(BF16)
    columns = lax.broadcasted_iota(jnp.int32, (width, count), 0)
    for step in range(2):
        value = jnp.where(columns == column, residuals[0, step : step + 1], 0.0)
        total = None
        for _ in range(3):
            part = value.astype(BF16)
            value = value - part.astype(F32)
            term = lax.dot_general(onto, part, (((1,), (1,)), ((), ())), preferred_element_type=F32)
            total = term if total is None else total + term
        spread[step] = total.reshape(rows, depth, width)

    for copy in copies:
        copy.wait()

    def row(x, _):
        own = q[x]
        free_p[x] = 2.0 * p[x] - later[0, x]
        free_q[x] = 2.0 * own - later[1, x] + spread[0, x]
        free_q2[x] = spread[1, x] - own
        mixed[x] = own * lap_p[x]
        return 0

    lax.fori_loop(0, rows, row, 0, unroll=8)


def full_kernel(lap_p, lap_q, mixed, now_q, pair, other, full_p, full_q, full_mixed):
    depth = lap_p.shape[1]
    half = pair.shape[0] // 2

    def add_p(span, layers, part):
        full_p[span, layers] = full_p[span, layers] + part
        full_mixed[span, layers] = full_mixed[span, layers] + now_q[span, layers] * part

    def add_q(span, layers, part):
        full_q[span, layers] = full_q[span, layers] + part

    for message, is_pair in ((pair, True), (other, False)):
        add_side(message.at[0:half], is_pair, depth, add_p)
        add_side(message.at[half:], is_pair, depth, add_q)


def step_kernel(plans, anchors, cells, amounts, free_p, free_q, full_p, full_q, *refs):
    tiles, (courant, p1, q1, pair, other_p, other_q) = refs[: len(plans) + 1], refs[len(plans) + 1 :]
    tile_rows = tiles[0].shape[0]
    for tile, place in zip(tiles, places(plans, anchors)):

        def put():
            speed = F32(SPACING_RATIO) * tile[...]
            factor = speed * speed * F32(1.0 / SCALE)
            span = pl.ds(place * tile_rows, tile_rows)
            courant[span] = factor
            p1[span] = free_p[span] + factor * full_p[span]
            q1[span] = free_q[span] + factor * full_q[span]

        pl.when((place >= 0) & (place < APT))(put)
    rows, depth, width = p1.shape
    half = rows // 2
    x0 = cells[0, 0]
    p1[x0] = p1[x0] + jnp.where(cell_mask(cells, depth, width), amounts[0, 0], 0.0)
    pair[0:half], other_p[...] = pack_rims(p1[...])
    pair[half:], other_q[...] = pack_rims(q1[...])


def places(plans, anchors):
    count = lax.axis_size("shot")
    me = lax.axis_index("shot")
    peers = [me] + [peer(me) for _, _, peer in plans]
    return [lax.rem(peer - anchors[0] + count, count) for peer in peers]


def inner_kernel(p1, along_y, along_xz, across, lap_p):
    put_laplacian(lap_p, p1[...], along_y, along_xz, across)


def image_kernel(
    plans, anchors, cells, amounts, q0, q1, courant, mixed, _, pair, other, full_p, *refs
):
    outs = refs
    rows, depth, width = q1.shape

    def add(span, layers, part):
        full_p[span, layers] = full_p[span, layers] + part

    add_side(pair.at[0 : rows // 2], True, depth, add)
    add_side(other, False, depth, add)

    x0 = cells[0, 0]
    here = cell_mask(cells, depth, width)
    added = q0[x0] * jnp.where(here, amounts[0, 0], 0.0) + q1[x0] * jnp.where(here, amounts[0, 1], 0.0)
    tile_rows = outs[0].shape[0]
    for out, place in zip(outs, places(plans, anchors)):
        inside = (place >= 0) & (place < APT)
        start = place * tile_rows

        def put():
            for row in range(tile_rows):
                x = start + row
                out[row] = courant[x] * (mixed[x] + q1[x] * full_p[x]) + jnp.where(x == x0, added, 0.0)

        def clear():
            out[...] = jnp.zeros(out.shape, F32)

        pl.when(inside)(put)
        pl.when(jnp.logical_not(inside))(clear)


def last_kernel(
    cells, amounts, p0, p1, q1, courant, lap_p, free_q2, along_y, along_xz, across, pair, other,
    forward_out, adjoint_out, p2, q2, lap_q, sems,
):
    rows, depth, width = p1.shape
    copies = []

    def save(field, out):
        copies.append(pltpu.make_async_copy(field, out, sems.at[len(copies)]))
        copies[-1].start()

    save(p1, forward_out.at[0, 0])
    save(q1, adjoint_out.at[0, 0])

    def row_p(x, _):
        p2[x] = 2.0 * p1[x] - p0[x] + courant[x] * lap_p[x]
        return 0

    lax.fori_loop(0, rows, row_p, 0, unroll=8)
    x0 = cells[0, 0]
    amount = jnp.where(cell_mask(cells, depth, width), amounts[0, 1], 0.0)
    p2[x0] = p2[x0] + amount
    save(p2, forward_out.at[0, 1])
    put_laplacian(lap_q, q1[...], along_y, along_xz, across)

    def add(span, layers, part):
        lap_q[span, layers] = lap_q[span, layers] + part

    add_side(pair.at[rows // 2 :], True, depth, add)
    add_side(other, False, depth, add)

    def row_q(x, _):
        q2[x] = 2.0 * q1[x] + free_q2[x] + courant[x] * lap_q[x]
        return 0

    lax.fori_loop(0, rows, row_q, 0, unroll=8)
    save(q2, adjoint_out.at[0, 1])
    for copy in copies:
        copy.wait()


def gradient_kernel(velocity, *refs):
    parts, out = refs[:-1], refs[-1]
    total = parts[0][...]
    for part in parts[1:]:
        total = total + part[...]
    out[...] = -(2.0 / velocity[...]) * total


def swap(message, start):
    ahead = [(i, i + 1) for i in range(start, lax.axis_size("sub") - 1, 2)]
    return lax.ppermute(message, "sub", ahead + [(i, j) for j, i in ahead])


def on_device(
    velocity, anchors, source_cells, receiver_cells, wavelet, residuals, forward_pair, adjoint_pair
):
    tile_rows, depth, width = velocity.shape
    rows = APT * tile_rows
    receiver_cells = jnp.transpose(receiver_cells, (1, 0, 2))
    field = (rows, depth, width)
    rims = (rows, 2 * RIM, width)
    plans = partners(lax.axis_size("shot"))
    plans_in = [plans[1], plans[2], *plans[3:], plans[0]] if len(plans) == 3 else plans

    arriving = [lax.ppermute(velocity, "shot", fetch) for fetch, _, _ in plans_in]

    pair, other, p0, q0, tile, cells, amounts = call(
        rims_kernel,
        [given(rims)] * 2 + [kept(field)] * 2 + [kept(velocity.shape)]
        + [pltpu.SMEM(a.shape, a.dtype) for a in (source_cells, wavelet)],
        [(IN_PLACE, in_hbm(a)) for a in (forward_pair, adjoint_pair, velocity, source_cells, wavelet)],
        out_specs=[IN_VMEM] * 5 + [IN_SMEM] * 2,
        scratch=[pltpu.SemaphoreType.DMA((2, 2)), pltpu.SemaphoreType.DMA((3,))],
        name="rims",
    )
    pair, other = swap(pair, 0), swap(other, 1)

    size = min(rows, 256 // depth) * depth
    operators = [
        pltpu.VMEM((2 * width, width), BF16),
        pltpu.VMEM((size, 2 * size), BF16),
        pltpu.VMEM((2, size, 2 * RIM * depth), BF16),
    ]
    free_p, lap_p, free_q, lap_q, free_q2, mixed, *operators = call(
        first_kernel,
        [kept(field)] * 6 + operators,
        [
            (IN_PLACE, in_hbm(receiver_cells)), (IN_PLACE, in_hbm(residuals)),
            (IN_PLACE, in_hbm(forward_pair)), (IN_PLACE, in_hbm(adjoint_pair)),
            (IN_VMEM, on_chip(p0)), (IN_VMEM, on_chip(q0)),
        ],
        scratch=[
            pltpu.VMEM((2,) + field, F32),
            pltpu.VMEM((2,) + field, F32),
            pltpu.VMEM(receiver_cells.shape, jnp.int32),
            pltpu.VMEM(residuals.shape, F32),
            pltpu.SemaphoreType.DMA((2, 2)),
            pltpu.SemaphoreType.DMA((2,)),
        ],
        name="first",
        cost=LONG,
    )
    scalars = [(IN_SMEM, on_smem(cells)), (IN_SMEM, on_smem(amounts))]

    full_p, full_q, mixed = call(
        full_kernel,
        [kept(field)] * 3,
        [(IN_VMEM, on_chip(a)) for a in (lap_p, lap_q, mixed, q0)] + [(IN_VMEM, pair), (IN_VMEM, other)],
        name="full",
        aliases={0: 0, 1: 1, 2: 2},
    )
    courant, p1, q1, pair, other_p, other_q = call(
        functools.partial(step_kernel, plans_in),
        [kept(field)] * 3 + [given(rims)] + [given((rows // 2, 2 * RIM, width))] * 2,
        [(IN_SMEM, anchors)] + scalars
        + [(IN_VMEM, on_chip(a)) for a in (free_p, free_q, full_p, full_q)]
        + [(IN_VMEM, on_chip(tile))]
        + [(IN_VMEM, other_tile) for other_tile in arriving],
        name="step",
    )
    pair, other_p, other_q = swap(pair, 0), swap(other_p, 1), swap(other_q, 1)

    (lap_p1,) = call(
        inner_kernel,
        [kept(field)],
        [(IN_VMEM, on_chip(a)) for a in (p1, *operators)],
        name="inner",
    )
    lap_p1, *images = call(
        functools.partial(image_kernel, plans),
        [kept(field)] + [given(velocity.shape)] * (len(plans) + 1),
        [(IN_SMEM, anchors)] + scalars
        + [(IN_VMEM, on_chip(a)) for a in (q0, q1, courant, mixed, lap_p1)]
        + [(IN_VMEM, pair), (IN_VMEM, other_p)],
        name="image",
        aliases={7: 0},
    )
    gathered = [images[0]] + [
        lax.ppermute(image, "shot", send) for image, (_, send, _) in zip(images[1:], plans)
    ]

    forward_out, adjoint_out = call(
        last_kernel,
        [given(forward_pair.shape), given(adjoint_pair.shape)],
        scalars
        + [(IN_VMEM, on_chip(a)) for a in (p0, p1, q1, courant, lap_p1, free_q2, *operators)]
        + [(IN_VMEM, pair), (IN_VMEM, other_q)],
        out_specs=[IN_PLACE, IN_PLACE],
        scratch=[pltpu.VMEM(field, F32)] * 3 + [pltpu.SemaphoreType.DMA((4,))],
        name="last",
        cost=LONG,
    )

    (gradient,) = call(
        gradient_kernel,
        [given(velocity.shape)],
        [(IN_VMEM, a) for a in (on_chip(tile), *gathered)],
        name="gradient",
    )
    return gradient, forward_out, adjoint_out


def solution(mesh):
    shot = ("grp", "shot")
    fields = P(shot, None, None, "sub", None)
    return jax.shard_map(
        on_device,
        mesh=mesh,
        in_specs=(
            P(shot, "sub", None),
            P(shot),
            P(shot, None),
            P(shot, None, None),
            P(shot, None),
            P(shot, None, None),
            fields,
            fields,
        ),
        out_specs=(P(shot, "sub", None), fields, fields),
        check_vma=False,
    )
```
